32 devices in a mesh: dp: 16 (over z, y, x), seq: 2 (over core).
Axes of the slice: x: 2, y: 2, z: 4, core: 2. Of those that a mesh axis runs over, the one named last changes fastest.
Arguments:
- patches: bfloat16 [4, 16, 512, 768], P(None, 'dp', 'seq'), may hold values from -6 to 6
- code_index: int32 [4, 16, 512], P(None, 'dp', 'seq'), may hold values from 0 to 50175
- lengths: int32 [4, 16, 8], P(None, 'dp'), may hold values from 0 to 512, as said below
- cotangent: bfloat16 [4, 16, 512, 768], P(None, 'dp', 'seq'), may hold values from -6 to 6
- codebook: bfloat16 [50176, 768], P('seq'), may hold values from -6 to 6
- first_gain: bfloat16 [768], P(('dp', 'seq')), may hold values from 0.099609375 to 1.8984375
- first_bias: bfloat16 [768], P(('dp', 'seq')), may hold values from -1.75 to 1.75
- project_weight: bfloat16 [768, 2304], P(('dp', 'seq')), may hold values from -0.21875 to 0.21875
- query_bias: bfloat16 [768], P(('dp', 'seq')), may hold values from -1.75 to 1.75
- value_bias: bfloat16 [768], P(('dp', 'seq')), may hold values from -1.75 to 1.75
- output_weight: bfloat16 [768, 768], P(('dp', 'seq')), may hold values from -1.75 to 1.75
- output_bias: bfloat16 [768], P(('dp', 'seq')), may hold values from -1.75 to 1.75
- second_gain: bfloat16 [768], P(('dp', 'seq')), may hold values from 0.099609375 to 1.8984375
- second_bias: bfloat16 [768], P(('dp', 'seq')), may hold values from -1.75 to 1.75
- up_weight: bfloat16 [768, 3072], P(('dp', 'seq')), may hold values from -0.21875 to 0.21875
- up_bias: bfloat16 [3072], P(('dp', 'seq')), may hold values from -1.75 to 1.75
- down_weight: bfloat16 [3072, 768], P(('dp', 'seq')), may hold values from -0.109375 to 0.109375
- down_bias: bfloat16 [768], P(('dp', 'seq')), may hold values from -1.75 to 1.75
Outputs:
- encoded: bfloat16 [4, 16, 512, 768], P(None, 'dp', 'seq')
- input_grad: bfloat16 [4, 16, 512, 768], P(None, 'dp', 'seq')
- grad_first_gain: float32 [768], P(('dp', 'seq'))
- grad_first_bias: float32 [768], P(('dp', 'seq'))
- grad_project_weight: float32 [768, 2304], P(('dp', 'seq'))
- grad_query_bias: float32 [768], P(('dp', 'seq'))
- grad_value_bias: float32 [768], P(('dp', 'seq'))
- grad_output_weight: float32 [768, 768], P(('dp', 'seq'))
- grad_output_bias: float32 [768], P(('dp', 'seq'))
- grad_second_gain: float32 [768], P(('dp', 'seq'))
- grad_second_bias: float32 [768], P(('dp', 'seq'))
- grad_up_weight: float32 [768, 3072], P(('dp', 'seq'))
- grad_up_bias: float32 [3072], P(('dp', 'seq'))
- grad_down_weight: float32 [3072, 768], P(('dp', 'seq'))
- grad_down_bias: float32 [768], P(('dp', 'seq'))
The draws below stay inside these ranges and needn't reach their ends.
Inputs may be any that keep to these rules, and one draw needn't show every extreme that they name: Each group's lengths are 64 but for at most one longer image; they sum to at most 512, and to exactly 512 in some group of every draw; in every group one image holds both row 255 and row 256.
All inputs are finite; a program needn't handle non-finite values.
Results may differ from the reference program's by a relative error of at most 0.0075.
Values may be sent and summed in bfloat16 or wider, within the bound.
No kernel may reach another device: no remote copies, remote signals or barrier semaphores. Data moves between devices by JAX's collectives and lax.ppermute only.
A program may use at most 256 MiB of HBM per device.

```python
import jax
import jax.numpy as jnp
from jax import lax

D = 768
HEADS = 12
HEAD_DIM = 64
FF = 3072
VOCAB = 50176
ROWS = 256
SHORT = 64
MB = 4
GROUPS = 16
PACK = 512
SLOTS = 8


def group_field(key, offset_scale, lowest, highest):
    parts = jax.random.split(key, 3)
    noise = jax.random.normal(parts[0], (MB, GROUPS, PACK, D), jnp.float32)
    offset = offset_scale * jax.random.normal(parts[1], (MB, GROUPS, 1, D), jnp.float32)
    factor = jnp.exp(jax.random.uniform(parts[2], (MB, GROUPS, 1, 1), jnp.float32, lowest, highest))
    return jnp.clip(factor * (noise + offset), -6.0, 6.0)


def draw_patches(key, part):
    key = jax.random.fold_in(key, 21)
    return group_field(key, 0.8, -1.0, 0.5).astype(jnp.bfloat16)


def draw_cotangent(key, part):
    key = jax.random.fold_in(key, 23)
    return group_field(key, 1.0, -1.5, 0.7).astype(jnp.bfloat16)


def draw_lengths(key, part):
    key = jax.random.fold_in(key, 11)
    keys = jax.random.split(key, 5)
    count = MB * GROUPS
    whole = jax.random.randint(keys[0], (count,), 0, 8) == 0
    forced = jax.random.randint(keys[1], (), 0, count)
    whole = whole | (jnp.arange(count, dtype=jnp.int32) == forced)
    before = jax.random.randint(keys[2], (count,), 0, ROWS // SHORT)
    start = before * SHORT
    middle = jax.random.randint(keys[3], (count,), ROWS - start + 1, ROWS - start + 2 * SHORT)
    room = (PACK - start - middle) // SHORT
    after = jax.random.randint(keys[4], (count,), 0, room + 1)
    places = jnp.arange(SLOTS, dtype=jnp.int32)[None, :]
    first_run = jnp.where(places < before[:, None], SHORT, 0)
    second_run = jnp.where((places > before[:, None]) & (places <= (before + after)[:, None]), SHORT, 0)
    picked = first_run + second_run + jnp.where(places == before[:, None], middle[:, None], 0)
    full_row = jnp.where(places == 0, PACK, 0)
    picked = jnp.where(whole[:, None], full_row, picked)
    return picked.reshape(MB, GROUPS, SLOTS).astype(jnp.int32)


def touch_ends(array, own_key, low, top_value):
    longest = array.shape.index(max(array.shape))
    spots = []
    for shift in (0, 1):
        where = [jax.random.randint(jax.random.fold_in(own_key, axis), (), 0, length) for axis, length in enumerate(array.shape)]
        where[longest] = (where[longest] + shift) % array.shape[longest]
        spots.append(tuple(where))
    return array.at[spots[0]].set(low).at[spots[1]].set(top_value)


def levels(rng, dims, shards, least, high):
    loudness, own = 1.0, jax.random.fold_in(rng, 6)
    for axis_at, blocks in shards:
        steps = jnp.exp(jax.random.uniform(jax.random.fold_in(own, axis_at), (blocks,), jnp.float32, least / len(shards), high / len(shards)))
        loudness = loudness * jnp.repeat(steps, dims[axis_at] // blocks).reshape([-1 if axis == axis_at else 1 for axis in range(len(dims))])
    return loudness


def gaussian(rng, dims, deviation, limit, cuts=(), held_as=jnp.bfloat16):
    loudness = levels(rng, dims, cuts, -0.22, 0.18) if cuts else 1.0
    array = jax.random.normal(rng, dims, jnp.float32) * deviation * loudness
    return jnp.minimum(jnp.maximum(array, -limit), limit).astype(held_as)


def setup_inputs(seed: int = 0) -> dict:
    arg_keys = jax.random.split(jax.random.key(seed), 19)
    return {
        "patches": draw_patches(jax.random.fold_in(arg_keys[18], 71), 0),
        "code_index": touch_ends(jax.random.randint(arg_keys[1], (MB, GROUPS, PACK), 0, VOCAB), jax.random.fold_in(arg_keys[1], 1), 0, VOCAB - 1).astype(jnp.int32),
        "lengths": draw_lengths(jax.random.fold_in(arg_keys[18], 71), 0),
        "cotangent": draw_cotangent(jax.random.fold_in(arg_keys[18], 71), 0),
        "codebook": gaussian(arg_keys[4], (VOCAB, D), 1.0, 6.0, ((0, 2),)),
        "first_gain": jnp.clip(1.0 + 0.18 * jax.random.normal(arg_keys[5], (D,), jnp.float32), 0.099609375, 1.8984375).astype(jnp.bfloat16),
        "first_bias": gaussian(arg_keys[6], (D,), 0.3, 1.75, ((0, 32),)),
        "project_weight": gaussian(arg_keys[7], (D, 3 * D), D ** -0.5, 0.21875, ((0, 32),)),
        "query_bias": gaussian(arg_keys[8], (D,), 0.3, 1.75, ((0, 32),)),
        "value_bias": gaussian(arg_keys[9], (D,), 0.3, 1.75, ((0, 32),)),
        "output_weight": gaussian(arg_keys[10], (D, D), (D // 64) ** -0.5, 1.75, ((0, 32),)),
        "output_bias": gaussian(arg_keys[11], (D,), 0.3, 1.75, ((0, 32),)),
        "second_gain": jnp.clip(1.0 + 0.18 * jax.random.normal(arg_keys[12], (D,), jnp.float32), 0.099609375, 1.8984375).astype(jnp.bfloat16),
        "second_bias": gaussian(arg_keys[13], (D,), 0.3, 1.75, ((0, 32),)),
        "up_weight": gaussian(arg_keys[14], (D, FF), D ** -0.5, 0.21875, ((0, 32),)),
        "up_bias": gaussian(arg_keys[15], (FF,), 0.3, 1.75, ((0, 32),)),
        "down_weight": gaussian(arg_keys[16], (FF, D), FF ** -0.5, 0.109375, ((0, 32),)),
        "down_bias": gaussian(arg_keys[17], (D,), 0.3, 1.75, ((0, 32),)),
    }


@jax.custom_vjp
def low(v):
    return lax.optimization_barrier(v.astype(jnp.bfloat16)).astype(jnp.float32)

@jax.custom_vjp
def low_back(v):
    return v

def low_keep(v):
    return (low(v), None)

def low_pass(kept, grad):
    return (grad,)

def back_keep(v):
    return (v, None)

def back_low(kept, grad):
    return (low(grad),)
low.defvjp(low_keep, low_pass)
low_back.defvjp(back_keep, back_low)
EPS = 1e-06
COMMIT = 0.5
HIGH = lax.Precision.HIGHEST

def norm_rows(values, gain, bias):
    mean = lax.optimization_barrier(jnp.mean(values, axis=-1, keepdims=True))
    centred = values - mean
    spread = lax.optimization_barrier(jnp.mean(centred * centred, axis=-1, keepdims=True))
    return centred * lax.rsqrt(spread + EPS) * gain + bias

def segment_rows(row_lengths):
    ends = jnp.cumsum(row_lengths).astype(jnp.int32)
    positions = jnp.arange(PACK, dtype=jnp.int32)
    return lax.optimization_barrier(jnp.sum((positions[:, None] >= ends[None, :]).astype(jnp.int32), axis=1))

def block(inputs, segments, params):
    first_gain, first_bias, project_weight, query_bias, value_bias, output_weight, output_bias, second_gain, second_bias, up_weight, up_bias, down_weight, down_bias = params
    scale = HEAD_DIM ** (-0.5)
    normed = low(norm_rows(inputs, first_gain, first_bias))
    bias_all = jnp.concatenate([query_bias, jnp.zeros_like(query_bias), value_bias])
    projected = low(low_back(jnp.dot(normed, project_weight, precision=HIGH) + bias_all))
    heads = projected.reshape(PACK, 3, HEADS, HEAD_DIM)
    queries, key_rows, value_rows = (heads[:, 0], heads[:, 1], heads[:, 2])
    scores = low_back(jnp.einsum('qhd,khd->hqk', queries, key_rows, precision=HIGH) * scale)
    allowed = (segments[:, None] == segments[None, :])[None]
    scores = jnp.where(allowed, scores, -1e+30)
    peak = lax.optimization_barrier(jnp.max(scores, axis=-1, keepdims=True))
    expo = jnp.exp(scores - peak)
    soft = low(expo / lax.optimization_barrier(jnp.sum(expo, axis=-1, keepdims=True)))
    mixed = jnp.einsum('hqk,khd->qhd', soft, value_rows, precision=HIGH).reshape(PACK, D)
    mixed = low(low_back(mixed))
    branch = low_back(jnp.dot(mixed, output_weight, precision=HIGH) + output_bias)
    resid = inputs + branch
    normed_two = low(norm_rows(resid, second_gain, second_bias))
    upper = low_back(jnp.dot(normed_two, up_weight, precision=HIGH) + up_bias)
    active = low(jax.nn.gelu(upper, approximate=True))
    lower = low_back(jnp.dot(active, down_weight, precision=HIGH) + down_bias)
    return resid + lower

def reference(patches, code_index, lengths, cotangent, codebook, first_gain, first_bias, project_weight, query_bias, value_bias, output_weight, output_bias, second_gain, second_bias, up_weight, up_bias, down_weight, down_bias):
    params = tuple((p.astype(jnp.float32) for p in (first_gain, first_bias, project_weight, query_bias, value_bias, output_weight, output_bias, second_gain, second_bias, up_weight, up_bias, down_weight, down_bias)))
    inputs = patches.astype(jnp.float32).reshape(MB * GROUPS, PACK, D)
    seg_all = jax.vmap(segment_rows)(lengths.reshape(MB * GROUPS, SLOTS))

    def forward(values_all, weights):

        def single(pack):
            values, segments = pack
            return block(values, segments, weights)
        return lax.map(jax.checkpoint(single), (values_all, seg_all))
    encoded, pullback = jax.vjp(forward, inputs, params)
    live = (seg_all < SLOTS).astype(jnp.float32)[..., None]
    table = codebook.astype(jnp.float32)
    quantized = jnp.take(table, code_index.reshape(-1).astype(jnp.int32), axis=0).reshape(MB * GROUPS, PACK, D)
    cot = cotangent.astype(jnp.float32).reshape(MB * GROUPS, PACK, D)
    grad_out = live * (cot + COMMIT * (encoded - quantized))
    grad_inputs, grads = pullback(grad_out)
    shape = (MB, GROUPS, PACK, D)
    out_encoded = (live * encoded).astype(jnp.bfloat16).reshape(shape)
    out_grad = grad_inputs.astype(jnp.bfloat16).reshape(shape)
    return (out_encoded, out_grad, grads[0], grads[1], grads[2], grads[3], grads[4], grads[5], grads[6], grads[7], grads[8], grads[9], grads[10], grads[11], grads[12])
```

```python
import functools

import jax
import jax.numpy as jnp
import numpy as np
from jax import lax
from jax.experimental import pallas as pl
from jax.experimental.pallas import tpu as pltpu
from jax.sharding import PartitionSpec as P

HEADS = 12
HEAD_DIM = 64
EPS = 1e-06
COMMIT = 0.5
SCALE = HEAD_DIM ** (-0.5)
NEGATIVE = -1e30
GELU_A = (2 / np.pi) ** 0.5
GELU_B = 0.044715
BOTH = ("dp", "seq")
F32 = jnp.float32
BF16 = jnp.bfloat16
ANY = pl.BlockSpec(memory_space=pl.ANY)
FIRST_GAIN, FIRST_BIAS, QUERY_BIAS, VALUE_BIAS, OUTPUT_BIAS = 0, 1, 2, 3, 4
SECOND_GAIN, SECOND_BIAS, DOWN_BIAS, UP_BIAS = 5, 6, 7, 8
SMALL = 256


def params():
    return pltpu.CompilerParams(vmem_limit_bytes=52 << 20)


def cost(flops, moved, exps=0):
    return pl.CostEstimate(flops=int(flops), bytes_accessed=int(moved), transcendentals=int(exps))


def nn(left, right):
    return jnp.dot(left, right, preferred_element_type=F32)


def nt(left, right):
    return lax.dot_general(left, right, (((1,), (1,)), ((), ())), preferred_element_type=F32)


def tn(left, right):
    return lax.dot_general(left, right, (((0,), (0,)), ((), ())), preferred_element_type=F32)


def stage_masks(chips, core):
    high = [1 << b for b in range(2, chips.bit_length() - 1)]
    return high + ([1, 2] if core == 0 else [2, 1])


def stage_count():
    return len(stage_masks(lax.axis_size("dp"), 0))


def relative_slots(chips, core):
    masks = stage_masks(chips, core)
    owners = []
    for s in range(chips):
        picked = [m for i, m in enumerate(masks) if s >> i & 1]
        owners.append(functools.reduce(lambda a, b: a ^ b, picked, 0))
    return np.array(owners, np.int32)


def slot_owner(core):
    chips = lax.axis_size("dp")
    rel = jnp.where(core == 0, relative_slots(chips, 0), relative_slots(chips, 1))
    return (rel ^ lax.axis_index("dp")).astype(jnp.int32)


def swap_cores(block):
    chips = lax.axis_size("dp")
    return lax.ppermute(
        block, BOTH, [(d * 2 + c, d * 2 + 1 - c) for d in range(chips) for c in (0, 1)]
    )


def swap_chips(block, stage):
    chips = lax.axis_size("dp")
    masks = [stage_masks(chips, core)[stage] for core in (0, 1)]
    return lax.ppermute(
        block, BOTH, [(d * 2 + c, (d ^ masks[c]) * 2 + c) for d in range(chips) for c in (0, 1)]
    )


class Gathered:
    def __init__(self, arrays, order, shape):
        self.arrays, self.order, self.shape = arrays, order, shape

    def specs(self):
        return [ANY] * len(self.arrays)

    def scratch(self):
        copies = sum(a.shape[0] for a in self.arrays) if len(self.arrays) > 1 else 1
        return [pltpu.VMEM(self.shape, BF16), pltpu.SemaphoreType.DMA((copies,))]


def fetch(order_ref, refs, weight, sems):
    if len(refs) == 1:
        copies = [pltpu.make_async_copy(refs[0], weight, sems.at[0])]
    else:
        per, rows, half = refs[0].shape
        copies = []
        for b, buf in enumerate(refs):
            for s in range(per):
                at = b * per + s
                row = pl.multiple_of(order_ref[at] * rows, 16)
                col = pl.multiple_of(order_ref[4 * per + b // 2] * half, 128)
                spot = weight.at[pl.ds(row, rows), pl.ds(col, half)]
                copies.append(pltpu.make_async_copy(buf.at[s], spot, sems.at[at]))
    for copy in copies:
        copy.start()
    for copy in copies:
        copy.wait()


def gather_rows(shard):
    chips = lax.axis_size("dp")
    core = lax.axis_index("seq")
    half = shard.shape[1] // 2
    rows = 2 * shard.shape[0]
    mine = lax.dynamic_slice_in_dim(shard, core * half, half, axis=1)
    theirs = lax.dynamic_slice_in_dim(shard, (1 - core) * half, half, axis=1)
    came = swap_cores(theirs)
    block = jnp.where(
        core == 0, jnp.concatenate([mine, came]), jnp.concatenate([came, mine])
    )[None]
    stages = stage_count()
    for stage in range(stages - 1):
        block = jnp.concatenate([block, swap_chips(block, stage)])
    low = swap_cores(block)
    last = swap_chips(block, stages - 1)
    high = swap_cores(last)
    shape = (chips * rows, 2 * half)
    order = jnp.concatenate(
        [slot_owner(core), slot_owner(1 - core), jnp.stack([core, 1 - core])]
    ).astype(jnp.int32)
    if rows % 16 == 0 and half % 128 == 0:
        return Gathered((block, last, low, high), order, shape)
    place = jnp.argsort(order[:chips]), jnp.argsort(order[chips : 2 * chips])
    own = jnp.take(jnp.concatenate([block, last]), place[0], axis=0)
    other = jnp.take(jnp.concatenate([low, high]), place[1], axis=0)
    own = own.reshape(chips * rows, half)
    other = other.reshape(chips * rows, half)
    full = jnp.where(
        core == 0, jnp.concatenate([own, other], 1), jnp.concatenate([other, own], 1)
    )
    return Gathered((full,), order, shape)


def merge_kernel(widths, order_ref, *refs):
    count = len(widths)
    send_ref, keep_ref = refs[-2:]
    at = 0
    for i, width in enumerate(widths):
        low, high, low_came, high_came = refs[4 * i : 4 * i + 4]
        spot = slice(at, at + width)
        keep_ref[:, :, spot] = (low[...].astype(F32) + low_came[...].astype(F32)).astype(BF16)
        send_ref[:, :, spot] = (high[...].astype(F32) + high_came[...].astype(F32)).astype(BF16)
        at += width


def merge(order, keeps, cames):
    chips = lax.axis_size("dp")
    half = chips // 2
    rows = keeps[0].shape[0] // chips
    widths = [k.shape[1] for k in keeps]
    operands, specs = [], []
    for keep, came, width in zip(keeps, cames, widths):
        for array in (keep, came):
            blocks = array.reshape(chips, rows, width)
            operands += [blocks, blocks]
            specs += [
                pl.BlockSpec((1, rows, width), lambda i, order: (order[i], 0, 0)),
                pl.BlockSpec((1, rows, width), lambda i, order: (order[i + half], 0, 0)),
            ]
    out = jax.ShapeDtypeStruct((half, rows, sum(widths)), BF16)
    out_spec = pl.BlockSpec((1, rows, sum(widths)), lambda i, order: (i, 0, 0))
    return pl.pallas_call(
        functools.partial(merge_kernel, widths),
        grid_spec=pltpu.PrefetchScalarGridSpec(
            num_scalar_prefetch=1, grid=(half,), in_specs=specs, out_specs=[out_spec, out_spec]
        ),
        out_shape=[out, out],
        compiler_params=params(),
        name="merge",
        cost_estimate=cost(sum(widths) * chips * rows, sum(widths) * chips * rows * 6),
    )(order, *operands)


def scatter_rows(sends, keeps):
    core = lax.axis_index("seq")
    send, keep = merge(slot_owner(core), keeps, [swap_cores(s) for s in sends])
    for stage in reversed(range(stage_count())):
        total = keep.astype(F32) + swap_chips(send, stage).astype(F32)
        count = total.shape[0] // 2
        send, keep = total[count:].astype(BF16), total[:count]
    keep = total[0]
    rows = keep.shape[0] // 2
    mine = lax.dynamic_slice_in_dim(keep, core * rows, rows, axis=0)
    theirs = lax.dynamic_slice_in_dim(keep, (1 - core) * rows, rows, axis=0)
    came = swap_cores(theirs)
    return mine, came


def by_half(mine, came):
    first = lax.axis_index("seq") == 0
    return jnp.concatenate([jnp.where(first, mine, came), jnp.where(first, came, mine)], axis=1)


def look_kernel(codes_ref, table_ref, out_ref, buf, sems):
    depth = buf.shape[0]
    table_rows = table_ref.shape[0]
    groups = out_ref.shape[0] // 16

    def start(g):
        slot = lax.rem(g, depth)
        for r in range(16):
            code = codes_ref[g * 16 + r]
            code = jnp.where(code < 0, code + table_rows, code)
            code = jnp.where(code >= table_rows, code - table_rows, code)
            first = lax.shift_left(lax.shift_right_logical(code, 4), 4)
            pltpu.make_async_copy(
                table_ref.at[pl.ds(pl.multiple_of(first, 16), 16), :],
                buf.at[slot, pl.ds(16 * r, 16), :],
                sems.at[slot],
            ).start()

    linear = lax.broadcasted_iota(jnp.int32, (16, 256), 0) * 256 + lax.broadcasted_iota(
        jnp.int32, (16, 256), 1
    )

    def finish(g):
        slot = lax.rem(g, depth)
        pick = jnp.zeros((16, 256), jnp.bool_)
        for r in range(16):
            code = codes_ref[g * 16 + r]
            held = (code >= 0) & (code < table_rows)
            pick = pick | (linear == jnp.where(held, r * 256 + r * 16 + (code & 15), -1))
        pltpu.make_async_copy(buf.at[slot], buf.at[slot], sems.at[slot]).wait()
        rows = nn(pick.astype(F32).astype(BF16), buf[slot])
        out_ref[pl.ds(pl.multiple_of(g * 16, 16), 16), :] = rows.astype(BF16)

    for g in range(depth - 1):
        start(jnp.int32(g))

    def step(g, carry):
        @pl.when(g + depth - 1 < groups)
        def _():
            start(g + depth - 1)

        finish(g)
        return carry

    lax.fori_loop(0, groups, step, 0)


def look_up(codes, table):
    count, width = codes.shape[0], table.shape[1]
    depth = 8
    return pl.pallas_call(
        look_kernel,
        grid_spec=pltpu.PrefetchScalarGridSpec(
            num_scalar_prefetch=1,
            grid=(1,),
            in_specs=[ANY],
            out_specs=pl.BlockSpec((count, width), lambda i, *_: (0, 0)),
            scratch_shapes=[
                pltpu.VMEM((depth, 256, width), BF16),
                pltpu.SemaphoreType.DMA((depth,)),
            ],
        ),
        out_shape=jax.ShapeDtypeStruct((count, width), BF16),
        compiler_params=params(),
        name="look_up",
        cost_estimate=cost(count * 512 * width, count * 32 * width),
    )(codes, table)


def norm_parts(values):
    mean = jnp.mean(values, axis=-1, keepdims=True)
    centred = values - mean
    spread = jnp.mean(centred * centred, axis=-1, keepdims=True)
    inverse = lax.rsqrt(spread + EPS)
    return centred * inverse, inverse


def norm_back(grad, normed, inverse, gain):
    c = grad * gain
    mean = jnp.mean(c, axis=-1, keepdims=True)
    along = jnp.mean(c * normed, axis=-1, keepdims=True)
    return inverse * (c - mean - normed * along)


def gelu_both(u):
    square = u * u
    t = jnp.tanh(u * (GELU_A + (GELU_A * GELU_B) * square))
    half = 0.5 + 0.5 * t
    slope = half + (0.5 * u) * (1.0 - t * t) * (GELU_A + (3 * GELU_A * GELU_B) * square)
    return u * half, slope


def column_sums(values):
    return jnp.sum(values.astype(F32), axis=0, keepdims=True)


def accumulate(ref, value):
    @pl.when(pl.program_id(0) == 0)
    def _():
        ref[...] = value

    @pl.when(pl.program_id(0) != 0)
    def _():
        ref[...] += value


def row_block(tile, columns):
    return pl.BlockSpec((tile, columns), lambda i, *_: (i, 0))


def whole(shape):
    return pl.BlockSpec(shape, lambda i, *_: (0,) * len(shape))


def shaped(dtype, *shape):
    return jax.ShapeDtypeStruct(shape, dtype)


def segment_of(position, lengths_ref, batch):
    end = jnp.int32(0)
    segment = jnp.zeros(position.shape, jnp.int32)
    for s in range(lengths_ref.shape[1]):
        end = end + lengths_ref[batch, s]
        segment = segment + (position >= end).astype(jnp.int32)
    return segment


def fill_mask(mask_ref, lengths_ref, core, batch):
    rows = mask_ref.shape[1]
    query = lax.broadcasted_iota(jnp.int32, (1, rows), 1) + core * rows
    query = segment_of(query, lengths_ref, batch)
    for part, owner in enumerate((core, 1 - core)):
        key = lax.broadcasted_iota(jnp.int32, (rows, 128), 0) + owner * rows
        key = segment_of(key, lengths_ref, batch)
        key = jnp.concatenate([key] * (rows // 128), axis=1)
        mask_ref[part * rows : (part + 1) * rows, :] = jnp.where(key == query, 0.0, NEGATIVE)


def head_lanes(block, head):
    lane = lax.broadcasted_iota(jnp.int32, block.shape, 1)
    return jnp.where((lane < HEAD_DIM) == (head == 0), block, jnp.zeros_like(block))


def attend_kernel(
    lengths_ref, core_ref, q_ref, k_ref, v_ref, k2_ref, v2_ref, o_ref, ot_ref, log_ref, mask_ref
):
    fill_mask(mask_ref, lengths_ref, core_ref[0], pl.program_id(0))
    for pair in range(q_ref.shape[1] // 128):
        at = slice(pair * 128, pair * 128 + 128)
        q = q_ref[:, at]
        k = jnp.concatenate([k_ref[:, at], k2_ref[:, at]], axis=0)
        values = jnp.concatenate([v_ref[:, at], v2_ref[:, at]], axis=0).T
        outs = []
        for head in range(2):
            score = nt(k, head_lanes(q, head)) + mask_ref[...]
            peak = jnp.max(score, axis=0, keepdims=True)
            expo = jnp.exp(score - peak)
            total = jnp.sum(expo, axis=0, keepdims=True)
            log_ref[0, pair, head : head + 1, :] = peak + jnp.log(total)
            here = slice(head * HEAD_DIM, head * HEAD_DIM + HEAD_DIM)
            outs.append(nn(values[here], expo.astype(BF16)) * (1.0 / total))
        out = jnp.concatenate(outs, axis=0)
        ot_ref[0, at, :] = out
        o_ref[:, at] = out.T.astype(BF16)


def attend(lengths, core, q, kv, kv2):
    micro = lengths.shape[0]
    rows, width = q.shape[0] // micro, q.shape[1]
    pairs = width // 128
    block = row_block(rows, width)
    values = pl.BlockSpec((rows, width), lambda b, *_: (b, 1))
    area = micro * HEADS * rows * 2 * rows
    return pl.pallas_call(
        attend_kernel,
        grid_spec=pltpu.PrefetchScalarGridSpec(
            num_scalar_prefetch=2,
            grid=(micro,),
            in_specs=[block, block, values, block, values],
            out_specs=[
                block,
                pl.BlockSpec((1, width, rows), lambda b, *_: (b, 0, 0)),
                pl.BlockSpec((1, pairs, 2, rows), lambda b, *_: (b, 0, 0, 0)),
            ],
            scratch_shapes=[pltpu.VMEM((2 * rows, rows), F32)],
        ),
        out_shape=[
            shaped(BF16, *q.shape),
            shaped(F32, micro, width, rows),
            shaped(F32, micro, pairs, 2, rows),
        ],
        compiler_params=params(),
        name="attend",
        cost_estimate=cost(area * HEAD_DIM * 16, q.size * 16, area),
    )(lengths, core, q, kv, kv, kv2, kv2)


def attend_back_kernel(
    lengths_ref,
    core_ref,
    q_ref,
    k_ref,
    v_ref,
    k2_ref,
    v2_ref,
    g_ref,
    ot_ref,
    log_ref,
    dq_ref,
    mine_ref,
    other_ref,
    mask_ref,
):
    rows = q_ref.shape[0]
    fill_mask(mask_ref, lengths_ref, core_ref[0], pl.program_id(0))
    for pair in range(q_ref.shape[1] // 128):
        at = slice(pair * 128, pair * 128 + 128)
        q = q_ref[:, at]
        g = g_ref[:, at]
        k = jnp.concatenate([k_ref[:, at], k2_ref[:, at]], axis=0)
        v = jnp.concatenate([v_ref[:, at], v2_ref[:, at]], axis=0)
        keys = k.T
        products = g.astype(F32).T * ot_ref[0, at, :]
        dq, dk, dv = [], 0.0, 0.0
        for head in range(2):
            here = slice(head * HEAD_DIM, head * HEAD_DIM + HEAD_DIM)
            q_head, g_head = head_lanes(q, head), head_lanes(g, head)
            p = jnp.exp(nt(k, q_head) + (mask_ref[...] - log_ref[0, pair, head : head + 1, :]))
            inner = jnp.sum(products[here], axis=0, keepdims=True)
            ds = (p * (nt(v, g_head) - inner)).astype(BF16)
            dq.append(nn(keys[here], ds))
            dk = dk + nn(ds, q_head)
            dv = dv + nn(p.astype(BF16), g_head)
        dq_ref[:, at] = (jnp.concatenate(dq, axis=0).T * SCALE).astype(BF16)
        for i, grad in enumerate((dk, dv)):
            mine_ref[i, :, at] = grad[:rows].astype(BF16)
            other_ref[i, :, at] = grad[rows:].astype(BF16)


def attend_back(lengths, core, q, kv, kv2, g, ot, logs):
    micro = lengths.shape[0]
    rows, width = q.shape[0] // micro, q.shape[1]
    pairs = width // 128
    block = row_block(rows, width)
    values = pl.BlockSpec((rows, width), lambda b, *_: (b, 1))
    both = pl.BlockSpec((2, rows, width), lambda b, *_: (0, b, 0))
    area = micro * HEADS * rows * 2 * rows
    return pl.pallas_call(
        attend_back_kernel,
        grid_spec=pltpu.PrefetchScalarGridSpec(
            num_scalar_prefetch=2,
            grid=(micro,),
            in_specs=[
                block,
                block,
                values,
                block,
                values,
                block,
                pl.BlockSpec((1, width, rows), lambda b, *_: (b, 0, 0)),
                pl.BlockSpec((1, pairs, 2, rows), lambda b, *_: (b, 0, 0, 0)),
            ],
            out_specs=[block, both, both],
            scratch_shapes=[pltpu.VMEM((2 * rows, rows), F32)],
        ),
        out_shape=[shaped(BF16, *q.shape)] + [shaped(BF16, 2, *q.shape)] * 2,
        compiler_params=params(),
        name="attend_back",
        cost_estimate=cost(area * HEAD_DIM * 40, q.size * 28, area),
    )(lengths, core, q, kv, kv, kv2, kv2, g, ot, logs)


def project_kernel(order_ref, x_ref, *refs):
    *sources, h_ref, q_ref, kv_ref, vec_ref, weight, sems = refs
    width = x_ref.shape[1]

    @pl.when(pl.program_id(0) == 0)
    def _():
        fetch(order_ref, sources, weight, sems)
        small = weight[:, 3 * width : 3 * width + 128].astype(F32).T
        vec_ref[...] = small[: vec_ref.shape[0]]

    vec = lambda i: vec_ref[i : i + 1, :]
    normed, _ = norm_parts(x_ref[...].astype(F32))
    h = (normed * vec(FIRST_GAIN) + vec(FIRST_BIAS)).astype(BF16)
    h_ref[...] = h
    q = (nn(h, weight[:, :width]) + vec(QUERY_BIAS)).astype(BF16)
    q_ref[...] = (q.astype(F32) * SCALE).astype(BF16)
    kv_ref[:, :width] = nn(h, weight[:, width : 2 * width]).astype(BF16)
    values = nn(h, weight[:, 2 * width : 3 * width]) + vec(VALUE_BIAS)
    kv_ref[:, width:] = values.astype(BF16)


def project(x, weight):
    rows, width = x.shape
    tile = 256
    block = row_block(tile, width)
    return pl.pallas_call(
        project_kernel,
        grid_spec=pltpu.PrefetchScalarGridSpec(
            num_scalar_prefetch=1,
            grid=(rows // tile,),
            in_specs=[block] + weight.specs(),
            out_specs=[block, block, row_block(tile, 2 * width), whole((16, width))],
            scratch_shapes=weight.scratch(),
        ),
        out_shape=[
            shaped(BF16, rows, width),
            shaped(BF16, rows, width),
            shaped(BF16, rows, 2 * width),
            shaped(F32, 16, width),
        ],
        compiler_params=params(),
        name="project",
        cost_estimate=cost(6 * rows * width * width, x.size * 10 + weight.shape[0] * 5120),
    )(weight.order, x, *weight.arrays)


def rise_kernel(order_ref, x_ref, o_ref, vec_ref, bias_ref, *refs):
    *sources, r_ref, h_ref, a_ref, s_ref, weight, sems = refs
    width = x_ref.shape[1]

    @pl.when(pl.program_id(0) == 0)
    def _():
        fetch(order_ref, sources, weight, sems)

    vec = lambda i: vec_ref[i : i + 1, :]
    r = x_ref[...].astype(F32) + nn(o_ref[...], weight[:, :width]) + vec(OUTPUT_BIAS)
    r_ref[...] = r
    normed, _ = norm_parts(r)
    h = (normed * vec(SECOND_GAIN) + vec(SECOND_BIAS)).astype(BF16)
    h_ref[...] = h
    for j in range(0, a_ref.shape[1], width):
        at = slice(j, j + width)
        u = nn(h, weight[:, width + j : 2 * width + j]) + bias_ref[:, at]
        active, slope = gelu_both(u)
        a_ref[:, at] = active.astype(BF16)
        s_ref[:, at] = slope.astype(BF16)


def rise(x, o, vec, bias, weight):
    rows, width = x.shape
    hidden = bias.shape[1]
    tile = 256
    block, wide = row_block(tile, width), row_block(tile, hidden)
    return pl.pallas_call(
        rise_kernel,
        grid_spec=pltpu.PrefetchScalarGridSpec(
            num_scalar_prefetch=1,
            grid=(rows // tile,),
            in_specs=[block, block, whole(vec.shape), whole(bias.shape)] + weight.specs(),
            out_specs=[block, block, wide, wide],
            scratch_shapes=weight.scratch(),
        ),
        out_shape=[
            shaped(F32, rows, width),
            shaped(BF16, rows, width),
            shaped(BF16, rows, hidden),
            shaped(BF16, rows, hidden),
        ],
        compiler_params=params(),
        name="rise",
        cost_estimate=cost(
            4 * rows * width * (width + hidden), rows * hidden * 8, rows * hidden
        ),
    )(weight.order, x, o, vec, bias, *weight.arrays)


def turn_kernel(
    order_ref, lengths_ref, core_ref, r_ref, a_ref, s_ref, cot_ref, near_ref, far_ref, vec_ref, *refs
):
    *sources, enc_ref, gz_ref, low_ref, gu_ref, db_ref, ub_ref, weight, sems = refs
    i = pl.program_id(0)
    rows, width = r_ref.shape

    @pl.when(i == 0)
    def _():
        fetch(order_ref, sources, weight, sems)

    filled = lengths_ref[i, 0]
    for s in range(1, lengths_ref.shape[1]):
        filled = filled + lengths_ref[i, s]
    position = lax.broadcasted_iota(jnp.int32, (rows, 1), 0) + core_ref[0] * rows
    live = (position < filled).astype(F32)
    z = r_ref[...] + nn(a_ref[...], weight[...]) + vec_ref[DOWN_BIAS : DOWN_BIAS + 1, :]
    enc_ref[...] = (live * z).astype(BF16)
    quantized = near_ref[...].astype(F32) + far_ref[...].astype(F32)
    gz = live * (cot_ref[...].astype(F32) + COMMIT * (z - quantized))
    gz_ref[...] = gz
    low = gz.astype(BF16)
    low_ref[...] = low
    accumulate(db_ref, column_sums(low))
    sums = []
    for j in range(0, a_ref.shape[1], width):
        at = slice(j, j + width)
        gu = (nt(low, weight[at, :]) * s_ref[:, at].astype(F32)).astype(BF16)
        gu_ref[:, at] = gu
        sums.append(column_sums(gu))
    accumulate(ub_ref, jnp.concatenate(sums, axis=1))


def turn(lengths, core, r, a, s, cot, near, far, vec, weight):
    rows, width = r.shape
    hidden = a.shape[1]
    tile = rows // lengths.shape[0]
    block, wide = row_block(tile, width), row_block(tile, hidden)
    return pl.pallas_call(
        turn_kernel,
        grid_spec=pltpu.PrefetchScalarGridSpec(
            num_scalar_prefetch=3,
            grid=(rows // tile,),
            in_specs=[block, wide, wide, block, block, block, whole(vec.shape)] + weight.specs(),
            out_specs=[block, block, block, wide, whole((1, width)), whole((1, hidden))],
            scratch_shapes=weight.scratch(),
        ),
        out_shape=[
            shaped(BF16, rows, width),
            shaped(F32, rows, width),
            shaped(BF16, rows, width),
            shaped(BF16, rows, hidden),
            shaped(F32, 1, width),
            shaped(F32, 1, hidden),
        ],
        compiler_params=params(),
        name="turn",
        cost_estimate=cost(8 * rows * width * hidden, rows * hidden * 10),
    )(weight.order, lengths, core, r, a, s, cot, near, far, vec, *weight.arrays)


def tall_kernel(core_ref, a_ref, g_ref, send_ref, keep_ref):
    out = tn(a_ref[...], g_ref[...]).astype(BF16)
    half = out.shape[1] // 2
    first = core_ref[0] == 0
    keep_ref[...] = jnp.where(first, out[:, :half], out[:, half:])
    send_ref[...] = jnp.where(first, out[:, half:], out[:, :half])


def tall_product(core, a, g):
    rows, hidden = a.shape
    width = g.shape[1]
    return pl.pallas_call(
        tall_kernel,
        grid_spec=pltpu.PrefetchScalarGridSpec(
            num_scalar_prefetch=1,
            grid=(hidden // width,),
            in_specs=[pl.BlockSpec((rows, width), lambda i, *_: (0, i)), whole(g.shape)],
            out_specs=[row_block(width, width // 2)] * 2,
        ),
        out_shape=[shaped(BF16, hidden, width // 2)] * 2,
        compiler_params=params(),
        name="tall_product",
        cost_estimate=cost(4 * rows * width * hidden, rows * hidden * 4),
    )(core, a, g)


def broad_kernel(core_ref, a_ref, g_ref, send_ref, keep_ref):
    i = pl.program_id(0)
    out = tn(a_ref[...], g_ref[...]).astype(BF16)

    @pl.when(i < pl.num_programs(0) // 2)
    def _():
        send_ref[...] = out

    @pl.when(i >= pl.num_programs(0) // 2)
    def _():
        keep_ref[...] = out


def broad_product(core, a, g, tiles):
    rows, width = a.shape
    columns = g.shape[1]
    tile = columns // tiles
    half = tiles // 2

    def column(i, core):
        return lax.rem(i + half * (1 - core[0]), tiles)

    return pl.pallas_call(
        broad_kernel,
        grid_spec=pltpu.PrefetchScalarGridSpec(
            num_scalar_prefetch=1,
            grid=(tiles,),
            in_specs=[
                whole(a.shape),
                pl.BlockSpec((rows, tile), lambda i, core: (0, column(i, core))),
            ],
            out_specs=[
                pl.BlockSpec((width, tile), lambda i, core: (0, jnp.minimum(i, half - 1))),
                pl.BlockSpec((width, tile), lambda i, core: (0, jnp.maximum(i - half, 0))),
            ],
        ),
        out_shape=[shaped(BF16, width, columns // 2)] * 2,
        compiler_params=params(),
        name="broad_product",
        cost_estimate=cost(4 * rows * width * columns, rows * columns * 4),
    )(core, a, g)


def fall_kernel(order_ref, gu_ref, gz_ref, r_ref, vec_ref, *refs):
    *sources, d_ref, low_ref, go_ref, gain_ref, bias_ref, ob_ref, weight, sems = refs
    width = r_ref.shape[1]

    @pl.when(pl.program_id(0) == 0)
    def _():
        fetch(order_ref, sources, weight, sems)

    e = nt(gu_ref[...], weight[:, width:])
    normed, inverse = norm_parts(r_ref[...])
    accumulate(gain_ref, column_sums(e * normed))
    accumulate(bias_ref, column_sums(e))
    d = gz_ref[...] + norm_back(e, normed, inverse, vec_ref[SECOND_GAIN : SECOND_GAIN + 1, :])
    d_ref[...] = d
    low = d.astype(BF16)
    low_ref[...] = low
    accumulate(ob_ref, column_sums(low))
    go_ref[...] = nt(low, weight[:, :width]).astype(BF16)


def fall(gu, gz, r, vec, weight):
    rows, width = r.shape
    hidden = gu.shape[1]
    tile = 256
    block = row_block(tile, width)
    return pl.pallas_call(
        fall_kernel,
        grid_spec=pltpu.PrefetchScalarGridSpec(
            num_scalar_prefetch=1,
            grid=(rows // tile,),
            in_specs=[row_block(tile, hidden), block, block, whole(vec.shape)] + weight.specs(),
            out_specs=[block] * 3 + [whole((1, width))] * 3,
            scratch_shapes=weight.scratch(),
        ),
        out_shape=[
            shaped(F32, rows, width),
            shaped(BF16, rows, width),
            shaped(BF16, rows, width),
        ]
        + [shaped(F32, 1, width)] * 3,
        compiler_params=params(),
        name="fall",
        cost_estimate=cost(4 * rows * width * (width + hidden), rows * hidden * 8),
    )(weight.order, gu, gz, r, vec, *weight.arrays)


def join_kernel(q_ref, mine_ref, came_ref, out_ref, qb_ref, vb_ref):
    width = q_ref.shape[1]
    out_ref[:, :width] = q_ref[...]
    accumulate(qb_ref, column_sums(q_ref[...]))
    for i in range(2):
        total = (mine_ref[i].astype(F32) + came_ref[i].astype(F32)).astype(BF16)
        out_ref[:, width * (i + 1) : width * (i + 2)] = total
    accumulate(vb_ref, column_sums(total))


def join(dq, mine, came):
    rows, width = dq.shape
    tile = 256
    both = pl.BlockSpec((2, tile, width), lambda i, *_: (0, i, 0))
    return pl.pallas_call(
        join_kernel,
        grid=(rows // tile,),
        in_specs=[row_block(tile, width), both, both],
        out_specs=[row_block(tile, 3 * width)] + [whole((1, width))] * 2,
        out_shape=[shaped(BF16, rows, 3 * width)] + [shaped(F32, 1, width)] * 2,
        compiler_params=params(),
        name="join",
        cost_estimate=cost(rows * width * 8, rows * width * 16),
    )(dq, mine, came)


def enter_kernel(order_ref, gp_ref, d_ref, x_ref, vec_ref, *refs):
    *sources, dx_ref, gain_ref, bias_ref, weight, sems = refs

    @pl.when(pl.program_id(0) == 0)
    def _():
        fetch(order_ref, sources, weight, sems)

    e = nt(gp_ref[...], weight[:, : gp_ref.shape[1]])
    normed, inverse = norm_parts(x_ref[...].astype(F32))
    accumulate(gain_ref, column_sums(e * normed))
    accumulate(bias_ref, column_sums(e))
    part = norm_back(e, normed, inverse, vec_ref[FIRST_GAIN : FIRST_GAIN + 1, :])
    dx_ref[...] = (d_ref[...] + part).astype(BF16)


def enter(gp, d, x, vec, weight):
    rows, width = x.shape
    tile = 256
    block = row_block(tile, width)
    return pl.pallas_call(
        enter_kernel,
        grid_spec=pltpu.PrefetchScalarGridSpec(
            num_scalar_prefetch=1,
            grid=(rows // tile,),
            in_specs=[row_block(tile, gp.shape[1]), block, block, whole(vec.shape)]
            + weight.specs(),
            out_specs=[block] + [whole((1, width))] * 2,
            scratch_shapes=weight.scratch(),
        ),
        out_shape=[shaped(BF16, rows, width)] + [shaped(F32, 1, width)] * 2,
        compiler_params=params(),
        name="enter",
        cost_estimate=cost(4 * rows * width * gp.shape[1], rows * width * 20),
    )(weight.order, gp, d, x, vec, *weight.arrays)


def body(
    patches,
    code_index,
    lengths,
    cotangent,
    codebook,
    first_gain,
    first_bias,
    project_weight,
    query_bias,
    value_bias,
    output_weight,
    output_bias,
    second_gain,
    second_bias,
    up_weight,
    up_bias,
    down_weight,
    down_bias,
):
    micro, _, local_rows, width = patches.shape
    rows = micro * local_rows
    hidden = up_weight.shape[1]
    place = lax.axis_index("seq")
    core = place.reshape(1).astype(jnp.int32)
    lengths = lengths[:, 0]
    shard_rows = project_weight.shape[0]
    spread = hidden // width

    small = [
        first_gain,
        first_bias,
        query_bias,
        value_bias,
        output_bias,
        second_gain,
        second_bias,
        down_bias,
    ]
    small = jnp.concatenate(
        [jnp.stack(small, axis=1), up_bias.reshape(shard_rows, spread)], axis=1
    )
    small = jnp.pad(small, ((0, 0), (0, SMALL - small.shape[1])))
    project_all = gather_rows(jnp.concatenate([project_weight, small], axis=1))
    wide_all = gather_rows(jnp.concatenate([output_weight, up_weight], axis=1))
    down_all = gather_rows(down_weight)

    codes = code_index.reshape(-1) - place * codebook.shape[0]
    far = swap_cores(look_up(swap_cores(code_index.reshape(-1)) - place * codebook.shape[0], codebook))
    near = look_up(codes, codebook)

    inputs = patches.reshape(rows, width)
    cotan = cotangent.reshape(rows, width)
    normed, q, kv, vec = project(inputs, project_all)
    bias_up = vec[UP_BIAS : UP_BIAS + spread].T.reshape(1, hidden)
    kv2 = swap_cores(kv)
    mixed, mixed_t, logs = attend(lengths, core, q, kv, kv2)
    resid, normed_two, active, slope = rise(inputs, mixed, vec, bias_up, wide_all)
    encoded, grad_z, grad_low, grad_upper, grad_down_bias, grad_up_bias = turn(
        lengths, core, resid, active, slope, cotan, near, far, vec, down_all
    )
    down_send, down_keep = tall_product(core, active, grad_low)
    grad_down = scatter_rows([down_send], [down_keep])
    up_send, up_keep = broad_product(core, normed_two, grad_upper, 4)
    grad_resid, branch_low, mixed_grad, grad_second_gain, grad_second_bias, grad_output_bias = fall(
        grad_upper, grad_z, resid, vec, wide_all
    )
    out_send, out_keep = broad_product(core, mixed, branch_low, 2)
    grad_wide = scatter_rows([out_send, up_send], [out_keep, up_keep])
    dq, mine, other = attend_back(lengths, core, q, kv, kv2, mixed_grad, mixed_t, logs)
    grad_project, grad_query_bias, grad_value_bias = join(dq, mine, swap_cores(other))
    project_send, project_keep = broad_product(core, normed, grad_project, 2)
    grad_inputs, grad_first_gain, grad_first_bias = enter(
        grad_project, grad_resid, inputs, vec, project_all
    )
    small = jnp.concatenate(
        [
            grad_first_gain,
            grad_first_bias,
            grad_query_bias,
            grad_value_bias,
            grad_output_bias,
            grad_second_gain,
            grad_second_bias,
            grad_down_bias,
            grad_up_bias.reshape(width, spread).T,
        ]
    )
    small = jnp.pad(small, ((0, SMALL // 2 - small.shape[0]), (0, 0))).T.astype(BF16)
    grad_project_all = scatter_rows([project_send, small], [project_keep, small])
    grad_small = grad_project_all[0][:, -SMALL // 2 :]

    grad_down = by_half(*grad_down)
    split = width // 2
    grad_output = by_half(*[g[:, :split] for g in grad_wide])
    grad_up = by_half(*[g[:, split:] for g in grad_wide])
    grad_project_weight = by_half(*[g[:, : -SMALL // 2] for g in grad_project_all])
    (
        grad_first_gain,
        grad_first_bias,
        grad_query_bias,
        grad_value_bias,
        grad_output_bias,
        grad_second_gain,
        grad_second_bias,
        grad_down_bias,
    ) = grad_small[:, :UP_BIAS].T
    grad_up_bias = grad_small[:, UP_BIAS : UP_BIAS + spread].reshape(-1)

    shape = patches.shape
    return (
        encoded.reshape(shape),
        grad_inputs.reshape(shape),
        grad_first_gain,
        grad_first_bias,
        grad_project_weight,
        grad_query_bias,
        grad_value_bias,
        grad_output,
        grad_output_bias,
        grad_second_gain,
        grad_second_bias,
        grad_up,
        grad_up_bias,
        grad_down,
        grad_down_bias,
    )


def solution(mesh):
    split = P(BOTH)
    split_rows = P(BOTH, None)
    patch = P(None, "dp", "seq", None)
    placed = (
        patch,
        P(None, "dp", "seq"),
        P(None, "dp", None),
        patch,
        P("seq", None),
        split,
        split,
        split_rows,
        split,
        split,
        split_rows,
        split,
        split,
        split,
        split_rows,
        split,
        split_rows,
        split,
    )
    return jax.shard_map(
        body,
        mesh=mesh,
        in_specs=placed,
        out_specs=(
            patch,
            patch,
            split,
            split,
            split_rows,
            split,
            split,
            split_rows,
            split,
            split,
            split,
            split_rows,
            split,
            split_rows,
            split,
        ),
        check_vma=False,
    )
```

```python
import functools

import jax
import jax.numpy as jnp
import numpy as np
from jax import lax
from jax.experimental import pallas as pl
from jax.experimental.pallas import tpu as pltpu
from jax.sharding import PartitionSpec as P

HEADS = 12
HEAD_DIM = 64
EPS = 1e-06
COMMIT = 0.5
SCALE = HEAD_DIM ** (-0.5)
NEGATIVE = -1e30
GELU_A = (2 / np.pi) ** 0.5
GELU_B = 0.044715
BOTH = ("dp", "seq")
F32 = jnp.float32
BF16 = jnp.bfloat16
ANY = pl.BlockSpec(memory_space=pl.ANY)
FIRST_GAIN, FIRST_BIAS, QUERY_BIAS, VALUE_BIAS, OUTPUT_BIAS = 0, 1, 2, 3, 4
SECOND_GAIN, SECOND_BIAS, DOWN_BIAS, UP_BIAS = 5, 6, 7, 8
SMALL = 256
GROUPS = ((0, 4), (4, 2))


def params():
    return pltpu.CompilerParams(vmem_limit_bytes=60 << 20)


def cost(micros):
    return pl.CostEstimate(flops=int(micros * 0.1e9), bytes_accessed=0, transcendentals=0)


def nn(left, right):
    return jnp.dot(left, right, preferred_element_type=F32)


def nt(left, right):
    return lax.dot_general(left, right, (((1,), (1,)), ((), ())), preferred_element_type=F32)


def tn(left, right):
    return lax.dot_general(left, right, (((0,), (0,)), ((), ())), preferred_element_type=F32)


def stage_masks(chips, core):
    bits = chips.bit_length() - 1
    high = [tuple(1 << b for b in range(at, min(at + 2, bits))) for at in range(2, bits, 2)]
    return high + ([(1,), (2,)] if core == 0 else [(2,), (1,)])


def stage_count():
    return len(stage_masks(lax.axis_size("dp"), 0))


def stage_partners(stage):
    chips = lax.axis_size("dp")
    both = [stage_masks(chips, core)[stage] for core in (0, 1)]
    picks = range(1, 1 << len(both[0]))
    return [tuple(sum(m for i, m in enumerate(masks) if p >> i & 1) for masks in both) for p in picks]


def flat_masks(core):
    return [m for stage in stage_masks(lax.axis_size("dp"), core) for m in stage]


def slot_owner(core):
    slot = jnp.arange(lax.axis_size("dp"), dtype=jnp.int32)
    owners = []
    for own in (0, 1):
        parts = [(slot >> i & 1) * m for i, m in enumerate(flat_masks(own))]
        owners.append(sum(parts) ^ lax.axis_index("dp"))
    return jnp.where(core == 0, owners[0], owners[1]).astype(jnp.int32)


def owner_slot(core):
    apart = jnp.arange(lax.axis_size("dp"), dtype=jnp.int32) ^ lax.axis_index("dp")
    slots = []
    for own in (0, 1):
        slots.append(sum(((apart & m) != 0) * (1 << i) for i, m in enumerate(flat_masks(own))))
    return jnp.where(core == 0, slots[0], slots[1]).astype(jnp.int32)


def swap_cores(block):
    chips = lax.axis_size("dp")
    return lax.ppermute(
        block, BOTH, [(d * 2 + c, d * 2 + 1 - c) for d in range(chips) for c in (0, 1)]
    )


def swap_chips(block, masks):
    chips = lax.axis_size("dp")
    pairs = [(d * 2 + c, (d ^ masks[c]) * 2 + c) for d in range(chips) for c in (0, 1)]
    return lax.ppermute(block, BOTH, pairs)


class Gathered:
    def __init__(self, arrays, shape, order=None, first=0):
        self.arrays, self.shape, self.first = arrays, shape, first
        self.order = jnp.zeros((1,), jnp.int32) if order is None else order

    def specs(self):
        return [ANY] * len(self.arrays)

    def scratch(self):
        return [pltpu.VMEM(self.shape, BF16), pltpu.SemaphoreType.DMA((32,))]

    def copies(self, order_ref, refs, weight, sems):
        copies = []
        if len(refs) == 1:
            rows, width = refs[0].shape[0], weight.shape[1]
            for j in range(weight.shape[0] // rows):
                source = refs[0].at[:, pl.ds(self.first + j * width, width)]
                spot = weight.at[pl.ds(j * rows, rows), :]
                copies.append(pltpu.make_async_copy(source, spot, sems.at[j]))
        else:
            per, rows, half = refs[0].shape
            for b, buf in enumerate(refs):
                for s in range(per):
                    at = b * per + s
                    row = pl.multiple_of(order_ref[at] * rows, 16)
                    col = pl.multiple_of(order_ref[4 * per + b // 2] * half, 128)
                    spot = weight.at[pl.ds(row, rows), pl.ds(col, half)]
                    copies.append(pltpu.make_async_copy(buf.at[s], spot, sems.at[at]))
        return copies


def after(value, *others):
    return lax.optimization_barrier((value, *others))[0]


class Gather:
    def __init__(self, shard):
        self.core = lax.axis_index("seq")
        self.half = shard.shape[1] // 2
        self.mine = lax.dynamic_slice_in_dim(shard, self.core * self.half, self.half, axis=1)
        theirs = lax.dynamic_slice_in_dim(shard, (1 - self.core) * self.half, self.half, axis=1)
        self.came = swap_cores(theirs)
        self.stage = -1
        places = [slot_owner(self.core), slot_owner(1 - self.core)]
        places.append(jnp.stack([self.core, 1 - self.core]).astype(jnp.int32))
        self.order = jnp.concatenate(places)

    def advance(self, *done):
        last = stage_count() - 1
        if self.stage < 0:
            came = after(self.came, *done)
            first, second = (self.mine, came), (came, self.mine)
            first, second = jnp.concatenate(first), jnp.concatenate(second)
            self.block = jnp.where(self.core == 0, first, second)[None]
        elif self.stage < last:
            came = [after(c, *done) for c in self.came]
            self.block = jnp.concatenate([self.block, *came])
        else:
            self.came = after(self.came[0], *done)
            self.high = swap_cores(self.came)
            return self.came
        self.stage += 1
        self.came = [swap_chips(self.block, masks) for masks in stage_partners(self.stage)]
        if self.stage == last:
            self.low = swap_cores(self.block)
        elif self.stage < last - 2:
            return self.advance()
        return self.block

    def result(self):
        chips, rows = 2 * self.block.shape[0], self.block.shape[1]
        shape = (chips * rows, 2 * self.half)
        core, order = self.core, self.order
        if rows % 16 == 0 and self.half % 128 == 0:
            return Gathered((self.block, self.came, self.low, self.high), shape, order)
        place = owner_slot(core), owner_slot(1 - core)
        own = jnp.take(jnp.concatenate([self.block, self.came]), place[0], axis=0)
        other = jnp.take(jnp.concatenate([self.low, self.high]), place[1], axis=0)
        own = own.reshape(chips * rows, self.half)
        other = other.reshape(chips * rows, self.half)
        full = jnp.where(
            core == 0, jnp.concatenate([own, other], 1), jnp.concatenate([other, own], 1)
        )
        return Gathered((full,), shape)


def add_kernel(count, parts, *refs):
    outs = refs[-parts:]
    at = 0
    for i in range(count):
        keep, came = refs[2 * i : 2 * i + 2]
        spot = slice(at, at + keep.shape[3])
        for j, out in enumerate(outs):
            out[:, :, spot] = (keep[j].astype(F32) + came[j].astype(F32)).astype(BF16)
        at += keep.shape[3]


def add_parts(keeps, cames, parts):
    slots, rows, _ = keeps[0].shape
    size = slots // parts
    steps = 2 if size > 1 else 1
    operands, specs = [], []
    for keep, came in zip(keeps, cames):
        width = keep.shape[2]
        operands += [a.reshape(parts, size, rows, width) for a in (keep, came)]
        specs += [pl.BlockSpec((parts, size // steps, rows, width), lambda i: (0, i, 0, 0))] * 2
    total = sum(k.shape[2] for k in keeps)
    out_spec = pl.BlockSpec((size // steps, rows, total), lambda i: (i, 0, 0))
    return pl.pallas_call(
        functools.partial(add_kernel, len(keeps), parts),
        grid=(steps,),
        in_specs=specs,
        out_specs=[out_spec] * parts,
        out_shape=[jax.ShapeDtypeStruct((size, rows, total), BF16)] * parts,
        compiler_params=params(),
        name="add_parts",
        cost_estimate=cost(1 + total * slots * rows * 1.3e-6),
    )(*operands)


class Scatter:
    def __init__(self, *pairs):
        self.keeps = [keep for _, keep in pairs]
        self.cames = [swap_cores(send) for send, _ in pairs]
        self.stage = stage_count()

    def advance(self, *done):
        cames = [after(came, *done) for came in self.cames]
        if self.stage == stage_count() or len(cames) == 1:
            self.stage -= 1
            if self.stage >= 0:
                partners = stage_partners(self.stage)
                keep, *sends = add_parts(self.keeps, cames, 1 + len(partners))
                self.keeps = [keep]
                self.cames = [swap_chips(s, masks) for s, masks in zip(sends, partners)]
                return keep
        total = self.keeps[0].astype(F32)
        for came in cames:
            total = total + came.astype(F32)
        if self.stage > 0:
            self.keeps, self.cames = [total.astype(BF16)], [jnp.zeros_like(total)]
            return self.advance()
        self.total = total[0]
        return self.total


def own_rows(part):
    core = lax.axis_index("seq")
    rows = part.shape[0] // 2
    mine = lax.dynamic_slice_in_dim(part, core * rows, rows, axis=0)
    theirs = lax.dynamic_slice_in_dim(part, (1 - core) * rows, rows, axis=0)
    return mine, swap_cores(theirs)


def by_half(mine, came):
    first = lax.axis_index("seq") == 0
    return jnp.concatenate([jnp.where(first, mine, came), jnp.where(first, came, mine)], axis=1)


def look_kernel(codes_ref, table_ref, out_ref, buf, sems):
    depth = buf.shape[0]
    table_rows = table_ref.shape[0]
    groups = out_ref.shape[0] // 16

    def start(g):
        slot = lax.rem(g, depth)
        for r in range(16):
            code = codes_ref[g * 16 + r]
            code = jnp.where(code < 0, code + table_rows, code)
            code = jnp.where(code >= table_rows, code - table_rows, code)
            first = lax.shift_left(lax.shift_right_logical(code, 4), 4)
            pltpu.make_async_copy(
                table_ref.at[pl.ds(pl.multiple_of(first, 16), 16), :],
                buf.at[slot, pl.ds(16 * r, 16), :],
                sems.at[slot],
            ).start()

    linear = lax.broadcasted_iota(jnp.int32, (16, 256), 0) * 256 + lax.broadcasted_iota(
        jnp.int32, (16, 256), 1
    )

    def finish(g):
        slot = lax.rem(g, depth)
        pick = jnp.zeros((16, 256), jnp.bool_)
        for r in range(16):
            code = codes_ref[g * 16 + r]
            held = (code >= 0) & (code < table_rows)
            pick = pick | (linear == jnp.where(held, r * 256 + r * 16 + (code & 15), -1))
        pltpu.make_async_copy(buf.at[slot], buf.at[slot], sems.at[slot]).wait()
        rows = nn(pick.astype(F32).astype(BF16), buf[slot])
        out_ref[pl.ds(pl.multiple_of(g * 16, 16), 16), :] = rows.astype(BF16)

    for g in range(depth - 1):
        start(jnp.int32(g))

    def step(g, carry):
        @pl.when(g + depth - 1 < groups)
        def _():
            start(g + depth - 1)

        finish(g)
        return carry

    lax.fori_loop(0, groups, step, 0)


def look_up(codes, table):
    count, width = codes.shape[0], table.shape[1]
    depth = 8
    return pl.pallas_call(
        look_kernel,
        grid_spec=pltpu.PrefetchScalarGridSpec(
            num_scalar_prefetch=1,
            grid=(1,),
            in_specs=[ANY],
            out_specs=pl.BlockSpec((count, width), lambda i, *_: (0, 0)),
            scratch_shapes=[
                pltpu.VMEM((depth, 256, width), BF16),
                pltpu.SemaphoreType.DMA((depth,)),
            ],
        ),
        out_shape=jax.ShapeDtypeStruct((count, width), BF16),
        compiler_params=params(),
        name="look_up",
        cost_estimate=cost(count * 0.0187),
    )(codes, table)


def norm_parts(values):
    mean = jnp.mean(values, axis=-1, keepdims=True)
    centred = values - mean
    spread = jnp.mean(centred * centred, axis=-1, keepdims=True)
    inverse = lax.rsqrt(spread + EPS)
    return centred * inverse, inverse


def norm_back(grad, normed, inverse, gain):
    c = grad * gain
    mean = jnp.mean(c, axis=-1, keepdims=True)
    along = jnp.mean(c * normed, axis=-1, keepdims=True)
    return inverse * (c - mean - normed * along)


def gelu_both(u):
    square = u * u
    t = jnp.tanh(u * (GELU_A + (GELU_A * GELU_B) * square))
    half = 0.5 + 0.5 * t
    slope = half + (0.5 * u) * (1.0 - t * t) * (GELU_A + (3 * GELU_A * GELU_B) * square)
    return u * half, slope


def column_sums(values):
    return jnp.sum(values.astype(F32), axis=0, keepdims=True)


def accumulate(ref, value):
    @pl.when(pl.program_id(0) == 0)
    def _():
        ref[...] = value

    @pl.when(pl.program_id(0) != 0)
    def _():
        ref[...] += value


def row_block(tile, columns):
    return pl.BlockSpec((tile, columns), lambda i, *_: (i, 0))


def whole(shape):
    return pl.BlockSpec(shape, lambda i, *_: (0,) * len(shape))


def shaped(dtype, *shape):
    return jax.ShapeDtypeStruct(shape, dtype)


def segment_of(position, lengths_ref, batch):
    end = jnp.int32(0)
    segment = jnp.zeros(position.shape, jnp.int32)
    for s in range(lengths_ref.shape[1]):
        end = end + lengths_ref[batch, s]
        segment = segment + (position >= end).astype(jnp.int32)
    return segment


def fill_mask(mask_ref, lengths_ref, core, batch):
    rows = mask_ref.shape[1]
    query = lax.broadcasted_iota(jnp.int32, (1, rows), 1) + core * rows
    query = segment_of(query, lengths_ref, batch)
    for part, owner in enumerate((core, 1 - core)):
        key = lax.broadcasted_iota(jnp.int32, (rows, 128), 0) + owner * rows
        key = segment_of(key, lengths_ref, batch)
        key = jnp.concatenate([key] * (rows // 128), axis=1)
        mask_ref[part * rows : (part + 1) * rows, :] = jnp.where(key == query, 0.0, NEGATIVE)


def head_lanes(block, head):
    lane = lax.broadcasted_iota(jnp.int32, block.shape, 1)
    return jnp.where((lane < HEAD_DIM) == (head == 0), block, jnp.zeros_like(block))


def attend_kernel(
    lengths_ref, core_ref, q_ref, k_ref, v_ref, k2_ref, v2_ref, o_ref, ot_ref, log_ref, mask_ref
):
    k_ref, v_ref, k2_ref, v2_ref = (ref.at[0] for ref in (k_ref, v_ref, k2_ref, v2_ref))
    fill_mask(mask_ref, lengths_ref, core_ref[0], pl.program_id(0))
    pairs = q_ref.shape[1] // 128

    def scores_of(pair):
        at = slice(pair * 128, pair * 128 + 128)
        k = jnp.concatenate([k_ref[:, at], k2_ref[:, at]], axis=0)
        return [nt(k, head_lanes(q_ref[:, at], head)) + mask_ref[...] for head in range(2)]

    ahead = scores_of(0)
    for pair in range(pairs):
        at = slice(pair * 128, pair * 128 + 128)
        values = jnp.concatenate([v_ref[:, at], v2_ref[:, at]], axis=0).T
        outs, scores = [], ahead
        if pair + 1 < pairs:
            ahead = scores_of(pair + 1)
        for head, score in enumerate(scores):
            peak = jnp.max(score, axis=0, keepdims=True)
            expo = jnp.exp(score - peak)
            total = jnp.sum(expo, axis=0, keepdims=True)
            log_ref[0, pair, head : head + 1, :] = peak + jnp.log(total)
            here = slice(head * HEAD_DIM, head * HEAD_DIM + HEAD_DIM)
            outs.append(nn(values[here], expo.astype(BF16)) * (1.0 / total))
        out = jnp.concatenate(outs, axis=0)
        ot_ref[0, at, :] = out
        o_ref[:, at] = out.T.astype(BF16)


def attend(lengths, core, q, kv, kv2):
    micro = lengths.shape[0]
    rows, width = q.shape[0] // micro, q.shape[1]
    pairs = width // 128
    block = row_block(rows, width)
    keys = pl.BlockSpec((1, rows, width), lambda b, *_: (0, b, 0))
    values = pl.BlockSpec((1, rows, width), lambda b, *_: (1, b, 0))
    area = micro * HEADS * rows * 2 * rows
    return pl.pallas_call(
        attend_kernel,
        grid_spec=pltpu.PrefetchScalarGridSpec(
            num_scalar_prefetch=2,
            grid=(micro,),
            in_specs=[block, keys, values, keys, values],
            out_specs=[
                block,
                pl.BlockSpec((1, width, rows), lambda b, *_: (b, 0, 0)),
                pl.BlockSpec((1, pairs, 2, rows), lambda b, *_: (b, 0, 0, 0)),
            ],
            scratch_shapes=[pltpu.VMEM((2 * rows, rows), F32)],
        ),
        out_shape=[
            shaped(BF16, *q.shape),
            shaped(F32, micro, width, rows),
            shaped(F32, micro, pairs, 2, rows),
        ],
        compiler_params=params(),
        name="attend",
        cost_estimate=cost(17),
    )(lengths, core, q, kv, kv, kv2, kv2)


def attend_back_kernel(
    first_batch,
    lengths_ref,
    core_ref,
    q_ref,
    k_ref,
    v_ref,
    k2_ref,
    v2_ref,
    g_ref,
    ot_ref,
    log_ref,
    *refs,
):
    dq_ref, mine_ref, other_ref, mask_ref = refs[-4:]
    rows = q_ref.shape[0]
    k_ref, v_ref, k2_ref, v2_ref = (ref.at[0] for ref in (k_ref, v_ref, k2_ref, v2_ref))
    fill_mask(mask_ref, lengths_ref, core_ref[0], pl.program_id(0) + first_batch)
    for pair in range(q_ref.shape[1] // 128):
        at = slice(pair * 128, pair * 128 + 128)
        q = q_ref[:, at]
        g = g_ref[:, at]
        k = jnp.concatenate([k_ref[:, at], k2_ref[:, at]], axis=0)
        v = jnp.concatenate([v_ref[:, at], v2_ref[:, at]], axis=0)
        keys = k.T
        products = g.astype(F32).T * ot_ref[0, at, :]
        dq, dk, dv = [], 0.0, 0.0
        for head in range(2):
            here = slice(head * HEAD_DIM, head * HEAD_DIM + HEAD_DIM)
            q_head, g_head = head_lanes(q, head), head_lanes(g, head)
            p = jnp.exp(nt(k, q_head) + (mask_ref[...] - log_ref[0, pair, head : head + 1, :]))
            inner = jnp.sum(products[here], axis=0, keepdims=True)
            ds = (p * (nt(v, g_head) - inner)).astype(BF16)
            dq.append(nn(keys[here], ds))
            dk = dk + nn(ds, q_head)
            dv = dv + nn(p.astype(BF16), g_head)
        dq_ref[:, at] = (jnp.concatenate(dq, axis=0).T * SCALE).astype(BF16)
        for i, grad in enumerate((dk, dv)):
            mine_ref[i, :, at] = grad[:rows].astype(BF16)
            other_ref[i, :, at] = grad[rows:].astype(BF16)


def attend_back(lengths, core, q, kv, kv2, g, ot, logs, group, batches, into=()):
    micro = lengths.shape[0]
    rows = q.shape[0] // micro
    first, pairs = group
    width = pairs * 128
    at = first // pairs
    start, stop = batches
    block = pl.BlockSpec((rows, width), lambda b, *_: (b + start, at))
    keys = pl.BlockSpec((1, rows, width), lambda b, *_: (0, b + start, at))
    values = pl.BlockSpec((1, rows, width), lambda b, *_: (1, b + start, at))
    both = pl.BlockSpec((2, rows, width), lambda b, *_: (0, b + start, 0))
    count = micro * rows
    operands = (lengths, core, q, kv, kv, kv2, kv2, g, ot, logs)
    return pl.pallas_call(
        functools.partial(attend_back_kernel, start),
        grid_spec=pltpu.PrefetchScalarGridSpec(
            num_scalar_prefetch=2,
            grid=(stop - start,),
            in_specs=[
                block,
                keys,
                values,
                keys,
                values,
                block,
                pl.BlockSpec((1, width, rows), lambda b, *_: (b + start, at, 0)),
                pl.BlockSpec((1, pairs, 2, rows), lambda b, *_: (b + start, at, 0, 0)),
            ]
            + [ANY] * len(into),
            out_specs=[pl.BlockSpec((rows, width), lambda b, *_: (b + start, 0)), both, both],
            scratch_shapes=[pltpu.VMEM((2 * rows, rows), F32)],
        ),
        out_shape=[shaped(BF16, count, width)] + [shaped(BF16, 2, count, width)] * 2,
        input_output_aliases={len(operands) + i: i for i in range(len(into))},
        compiler_params=params(),
        name="attend_back",
        cost_estimate=cost(1.2 * pairs * (stop - start)),
    )(*operands, *into)


def project_kernel(weight_in, order_ref, x_ref, *refs):
    *sources, h_ref, q_ref, kv_ref, vec_ref, full_ref, weight, sems, full_sem = refs
    width = x_ref.shape[1]
    i = pl.program_id(0)
    full_copy = pltpu.make_async_copy(weight, full_ref, full_sem)

    @pl.when(i == 0)
    def _():
        copies = weight_in.copies(order_ref, sources, weight, sems)
        for copy in copies:
            copy.start()
        for copy in copies:
            copy.wait()
        full_copy.start()
        small = weight[:, 3 * width : 3 * width + 128].astype(F32).T
        vec_ref[...] = small[: vec_ref.shape[0]]

    vec = lambda i: vec_ref[i : i + 1, :]
    normed, _ = norm_parts(x_ref[...].astype(F32))
    h = (normed * vec(FIRST_GAIN) + vec(FIRST_BIAS)).astype(BF16)
    h_ref[...] = h
    q = (nn(h, weight[:, :width]) + vec(QUERY_BIAS)).astype(BF16)
    q_ref[...] = (q.astype(F32) * SCALE).astype(BF16)
    kv_ref[0] = nn(h, weight[:, width : 2 * width]).astype(BF16)
    values = nn(h, weight[:, 2 * width : 3 * width]) + vec(VALUE_BIAS)
    kv_ref[1] = values.astype(BF16)

    @pl.when(i == pl.num_programs(0) - 1)
    def _():
        full_copy.wait()


def project(x, weight):
    rows, width = x.shape
    tile = 256
    block = row_block(tile, width)
    return pl.pallas_call(
        functools.partial(project_kernel, weight),
        grid_spec=pltpu.PrefetchScalarGridSpec(
            num_scalar_prefetch=1,
            grid=(rows // tile,),
            in_specs=[block] + weight.specs(),
            out_specs=[
                block,
                block,
                pl.BlockSpec((2, tile, width), lambda i, *_: (0, i, 0)),
                whole((16, width)),
                ANY,
            ],
            scratch_shapes=weight.scratch() + [pltpu.SemaphoreType.DMA],
        ),
        out_shape=[
            shaped(BF16, rows, width),
            shaped(BF16, rows, width),
            shaped(BF16, 2, rows, width),
            shaped(F32, 16, width),
            shaped(BF16, *weight.shape),
        ],
        compiler_params=params(),
        name="project",
        cost_estimate=cost(10),
    )(weight.order, x, *weight.arrays)


def store_rows(ref, slot_ref, first, value, at=0):
    value = value.astype(BF16)
    columns = slice(at, at + value.shape[1])
    if len(ref.shape) == 2:
        ref[:, columns] = value
        return
    chips, rows, _ = ref.shape
    for chip in range(chips):
        ref[slot_ref[first + chip], :, columns] = value[chip * rows : chip * rows + rows]


def by_slots(chips, rows):
    return rows // chips % 16 == 0


def in_slots(product, slots):
    chips = slots.shape[0]
    if product.ndim == 3:
        return product
    product = product.reshape(chips, -1, product.shape[1])
    return jnp.zeros_like(product).at[slots].set(product)


def pair_in_slots(slots, send, keep):
    chips = slots.shape[0] // 2
    return in_slots(send, slots[chips:]), in_slots(keep, slots[:chips])


def product_shape(chips, rows, columns):
    if by_slots(chips, rows):
        return (chips, rows // chips, columns)
    return (rows, columns)


def product_spec(chips, rows, columns, index):
    lead = (0, 0) if by_slots(chips, rows) else (0,)
    return pl.BlockSpec(
        product_shape(chips, rows, columns), lambda i, *_: lead + (index(i),)
    )


def mlp_kernel(
    wide_in,
    down_in,
    lengths_ref,
    core_ref,
    slot_ref,
    x_ref,
    o_ref,
    cot_ref,
    near_ref,
    near2_ref,
    far_ref,
    far2_ref,
    vec_ref,
    source_ref,
    enc_ref,
    d_ref,
    go_ref,
    down_send_ref,
    down_keep_ref,
    up_send_ref,
    up_keep_ref,
    out_send_ref,
    out_keep_ref,
    db_ref,
    ub_ref,
    gain_ref,
    bias_ref,
    ob_ref,
    wide,
    down,
    active_all,
    upper_all,
    normed_all,
    z_all,
    low_all,
    slope_tile,
    wide_sems,
    down_sems,
):
    i = pl.program_id(0)
    tiles = lengths_ref.shape[0]
    rows, width = x_ref.shape
    blocks = active_all.shape[0]
    core = core_ref[0]
    chips = slot_ref.shape[0] // 2
    wide_copies = wide_in.copies(None, [source_ref], wide, wide_sems)
    down_copies = down_in.copies(None, [source_ref], down, down_sems)

    @pl.when(i == 0)
    def _():
        for copy in wide_copies + down_copies:
            copy.start()
        for copy in wide_copies:
            copy.wait()

    def up_columns(b):
        return wide[:, width * (b + 1) : width * (b + 2)]

    def down_rows(b):
        return down[width * b : width * (b + 1), :]

    @pl.when(i < tiles)
    def _():
        at = pl.ds(pl.multiple_of(i * rows, rows), rows)
        vec = lambda k: vec_ref[k : k + 1, :]
        r = x_ref[...].astype(F32) + nn(o_ref[at, :], wide[:, :width]) + vec(OUTPUT_BIAS)
        normed, inverse = norm_parts(r)
        h = (normed * vec(SECOND_GAIN) + vec(SECOND_BIAS)).astype(BF16)
        normed_all[at, :] = h

        def rise(b):
            return nn(h, up_columns(b)) + vec(UP_BIAS + b)

        upper = rise(0)
        for b in range(blocks):
            now = upper
            if b + 1 < blocks:
                upper = rise(b + 1)
            active, slope = gelu_both(now)
            active_all[b, at, :] = active.astype(BF16)
            slope_tile[b] = slope.astype(BF16)

        @pl.when(i == 0)
        def _():
            for copy in down_copies:
                copy.wait()

        filled = lengths_ref[i, 0]
        for k in range(1, lengths_ref.shape[1]):
            filled = filled + lengths_ref[i, k]
        position = lax.broadcasted_iota(jnp.int32, (rows, 1), 0) + core * rows
        live = (position < filled).astype(F32)
        z = r + vec(DOWN_BIAS)
        for b in range(blocks):
            z = z + nn(active_all[b, at, :], down_rows(b))
        enc_ref[...] = (live * z).astype(BF16)
        early = i < tiles // 2
        near = jnp.where(early, near_ref[...], near2_ref[...]).astype(F32)
        far = jnp.where(early, far_ref[...], far2_ref[...]).astype(F32)
        gz = live * (cot_ref[...].astype(F32) + COMMIT * (z - (near + far)))
        low = gz.astype(BF16)
        z_all[at, :] = low
        accumulate(db_ref, column_sums(low))
        sums = []
        e = 0.0
        fall = nt(low, down_rows(0))
        for b in range(blocks):
            now = fall
            if b + 1 < blocks:
                fall = nt(low, down_rows(b + 1))
            gu = (now * slope_tile[b].astype(F32)).astype(BF16)
            upper_all[b, at, :] = gu
            sums.append(column_sums(gu))
            e = e + nt(gu, up_columns(b))
        accumulate(ub_ref, jnp.concatenate(sums, axis=1))
        accumulate(gain_ref, column_sums(e * normed))
        accumulate(bias_ref, column_sums(e))
        d = gz + norm_back(e, normed, inverse, vec(SECOND_GAIN))
        d_ref[...] = d
        low = d.astype(BF16)
        low_all[at, :] = low
        accumulate(ob_ref, column_sums(low))
        go_ref[...] = nt(low, wide[:, :width]).astype(BF16)

    def split(out, send_ref, keep_ref):
        half = out.shape[1] // 2
        first = core == 0
        store_rows(keep_ref, slot_ref, 0, jnp.where(first, out[:, :half], out[:, half:]))
        store_rows(send_ref, slot_ref, chips, jnp.where(first, out[:, half:], out[:, :half]))

    for j in range(blocks):

        @pl.when(i == tiles + j)
        def _():
            split(tn(active_all[j], z_all[...]), down_send_ref, down_keep_ref)
            column = lax.rem(j + blocks // 2 * (1 - core), blocks)
            product = tn(normed_all[...], upper_all[column])
            if j < blocks // 2:
                store_rows(up_send_ref, slot_ref, chips, product)
            else:
                store_rows(up_keep_ref, slot_ref, 0, product)
            if j == blocks - 1:
                split(tn(o_ref[...], low_all[...]), out_send_ref, out_keep_ref)


def mlp(lengths, core, slots, x, o, cot, near, far, vec, wide, down):
    rows, width = x.shape
    hidden = down.shape[0]
    tiles, blocks = lengths.shape[0], hidden // width
    tile = rows // tiles
    chips = slots.shape[0] // 2
    block = pl.BlockSpec((tile, width), lambda i, *_: (jnp.minimum(i, tiles - 1), 0))
    early = pl.BlockSpec((tile, width), lambda i, *_: (jnp.minimum(i, tiles // 2 - 1), 0))
    late = pl.BlockSpec(
        (tile, width), lambda i, *_: (jnp.clip(i - tiles // 2, 0, tiles // 2 - 1), 0)
    )
    row, long_row = whole((1, width)), whole((1, hidden))
    down_spec = product_spec(chips, width, width // 2, lambda i: jnp.maximum(i - tiles, 0))
    send_spec = product_spec(chips, width, width, lambda i: jnp.clip(i - tiles, 0, blocks // 2 - 1))
    keep_spec = product_spec(chips, width, width, lambda i: jnp.maximum(i - tiles - blocks // 2, 0))
    out_spec = product_spec(chips, width, width // 2, lambda i: 0)
    half_hidden = shaped(BF16, *product_shape(chips, width, hidden // 2))
    half_width = shaped(BF16, *product_shape(chips, width, width // 2))
    results = pl.pallas_call(
        functools.partial(mlp_kernel, wide, down),
        grid_spec=pltpu.PrefetchScalarGridSpec(
            num_scalar_prefetch=3,
            grid=(tiles + blocks,),
            in_specs=[block, whole(o.shape), block, early, late, early, late]
            + [whole(vec.shape), ANY],
            out_specs=[block, block, block]
            + [down_spec, down_spec, send_spec, keep_spec, out_spec, out_spec]
            + [row, long_row, row, row, row],
            scratch_shapes=[
                pltpu.VMEM(wide.shape, BF16),
                pltpu.VMEM(down.shape, BF16),
                pltpu.VMEM((blocks, rows, width), BF16),
                pltpu.VMEM((blocks, rows, width), BF16),
                pltpu.VMEM((rows, width), BF16),
                pltpu.VMEM((rows, width), BF16),
                pltpu.VMEM((rows, width), BF16),
                pltpu.VMEM((blocks, tile, width), BF16),
                pltpu.SemaphoreType.DMA((blocks,)),
                pltpu.SemaphoreType.DMA((blocks,)),
            ],
        ),
        out_shape=[
            shaped(BF16, rows, width),
            shaped(F32, rows, width),
            shaped(BF16, rows, width),
            half_hidden,
            half_hidden,
            half_hidden,
            half_hidden,
            half_width,
            half_width,
            shaped(F32, 1, width),
            shaped(F32, 1, hidden),
            shaped(F32, 1, width),
            shaped(F32, 1, width),
            shaped(F32, 1, width),
        ],
        compiler_params=params(),
        name="mlp",
        cost_estimate=cost(55),
    )(lengths, core, slots, x, o, cot, *near, *far, vec, *wide.arrays)
    down_pair, up_pair, out_pair = (pair_in_slots(slots, *results[k : k + 2]) for k in (3, 5, 7))
    return results[:3], down_pair, up_pair, out_pair, results[9:]


def leave_kernel(group, last, core_ref, slot_ref, *refs):
    refs = list(refs)
    take = lambda count: [refs.pop(0) for _ in range(count)]
    dq_ref, mine_ref, came_ref, h_ref, full_ref = take(5)
    if last:
        e_in_ref, d_ref, x_ref, vec_ref, small_ref = take(5)
        send_ref, keep_ref, dx_ref = take(3)
        sums = take(1)[0]
    else:
        send_ref, keep_ref, e_ref, sums = take(4)
    weight, grads, sems = refs
    first, pairs = group
    size = pairs * 128
    i = pl.program_id(0)
    rows = dq_ref.shape[0]
    width = h_ref.shape[1]
    core = core_ref[0]
    chips = slot_ref.shape[0] // 2
    copies = []
    for part in range(3):
        source = full_ref.at[:, pl.ds(part * width + first * 128, size)]
        spot = weight.at[:, pl.ds(part * size, size)]
        copies.append(pltpu.make_async_copy(source, spot, sems.at[part]))

    @pl.when(i == 0)
    def _():
        for copy in copies:
            copy.start()
        for copy in copies:
            copy.wait()
        sums[...] = jnp.zeros(sums.shape, F32)

    @pl.when(i < pl.num_programs(0) - 1)
    def _():
        at = pl.ds(pl.multiple_of(i * rows, rows), rows)
        here = slice(first * 128, first * 128 + size)
        dq = dq_ref[...]
        parts = [dq]
        for k in range(2):
            total = mine_ref[k].astype(F32) + came_ref[k].astype(F32)
            parts.append(total.astype(BF16))
        sums[QUERY_BIAS : QUERY_BIAS + 1, here] += column_sums(dq)
        sums[VALUE_BIAS : VALUE_BIAS + 1, here] += column_sums(parts[2])
        grad = jnp.concatenate(parts, axis=1)
        half = grad.shape[1] // 2
        grads[0, at, :] = grad[:, :half]
        grads[1, at, :] = grad[:, half:]
        e = nt(grad, weight[...])
        if last:
            e = e + e_in_ref[...]
            normed, inverse = norm_parts(x_ref[...].astype(F32))
            sums[FIRST_GAIN : FIRST_GAIN + 1, :] += column_sums(e * normed)
            sums[FIRST_BIAS : FIRST_BIAS + 1, :] += column_sums(e)
            back = norm_back(e, normed, inverse, vec_ref[FIRST_GAIN : FIRST_GAIN + 1, :])
            dx_ref[...] = (d_ref[...] + back).astype(BF16)
        else:
            e_ref[...] = e

    @pl.when(i == pl.num_programs(0) - 1)
    def _():
        store_rows(send_ref, slot_ref, chips, tn(h_ref[...], grads[1 - core]))
        store_rows(keep_ref, slot_ref, 0, tn(h_ref[...], grads[core]))
        if last:
            small = sums[...] + small_ref[...]
            small = jnp.concatenate([small, jnp.zeros((SMALL // 2 - 16, width), F32)]).T
            store_rows(send_ref, slot_ref, chips, small, grads.shape[2])
            store_rows(keep_ref, slot_ref, 0, small, grads.shape[2])


def leave(group, core, slots, dq, mine, came, h, full, *rest):
    rows, width = h.shape
    size = dq.shape[1]
    last = bool(rest)
    tile = 256
    tiles = rows // tile
    chips = slots.shape[0] // 2
    half = 3 * size // 2
    columns = half + (SMALL // 2 if last else 0)

    def part(columns):
        return pl.BlockSpec((tile, columns), lambda i, *_: (jnp.minimum(i, tiles - 1), 0))

    both = pl.BlockSpec((2, tile, size), lambda i, *_: (0, jnp.minimum(i, tiles - 1), 0))
    block = part(width)
    in_specs = [part(size), both, both, whole(h.shape), ANY]
    if last:
        in_specs += [block, block, block, whole(rest[3].shape), whole(rest[4].shape)]
    product = product_spec(chips, width, columns, lambda i: 0)
    product_out = shaped(BF16, *product_shape(chips, width, columns))
    send, keep, out, sums = pl.pallas_call(
        functools.partial(leave_kernel, group, last),
        grid_spec=pltpu.PrefetchScalarGridSpec(
            num_scalar_prefetch=2,
            grid=(tiles + 1,),
            in_specs=in_specs,
            out_specs=[product, product, block, whole((16, width))],
            scratch_shapes=[
                pltpu.VMEM((width, 3 * size), BF16),
                pltpu.VMEM((2, rows, half), BF16),
                pltpu.SemaphoreType.DMA((3,)),
            ],
        ),
        out_shape=[
            product_out,
            product_out,
            shaped(BF16 if last else F32, rows, width),
            shaped(F32, 16, width),
        ],
        compiler_params=params(),
        name="leave",
        cost_estimate=cost(13),
    )(core, slots, dq, mine, came, h, full, *rest)
    return pair_in_slots(slots, send, keep), out, sums


def body(
    patches,
    code_index,
    lengths,
    cotangent,
    codebook,
    first_gain,
    first_bias,
    project_weight,
    query_bias,
    value_bias,
    output_weight,
    output_bias,
    second_gain,
    second_bias,
    up_weight,
    up_bias,
    down_weight,
    down_bias,
):
    micro, _, local_rows, width = patches.shape
    rows = micro * local_rows
    hidden = up_weight.shape[1]
    place = lax.axis_index("seq")
    core = place.reshape(1).astype(jnp.int32)
    lengths = lengths[:, 0]
    shard_rows = project_weight.shape[0]
    spread = hidden // width

    small = [
        first_gain,
        first_bias,
        query_bias,
        value_bias,
        output_bias,
        second_gain,
        second_bias,
        down_bias,
    ]
    small += [up_bias[j * shard_rows : (j + 1) * shard_rows] for j in range(spread)]
    line = lax.broadcasted_iota(jnp.int32, (16, shard_rows), 0)
    table = jnp.zeros((16, shard_rows), BF16)
    for j, vector in enumerate(small):
        table = jnp.where(line == j, vector[None, :], table)
    small = jnp.pad(table.T, ((0, 0), (0, SMALL - 16)))
    g1 = Gather(jnp.concatenate([project_weight, small], axis=1))
    inputs = patches.reshape(rows, width)
    cotan = cotangent.reshape(rows, width)
    codes = code_index.reshape(-1)
    local = codes - place * codebook.shape[0]
    asked = swap_cores(codes) - place * codebook.shape[0]
    piece = rows // 2
    asked = [asked[i : i + piece] for i in range(0, rows, piece)]
    local = [local[i : i + piece] for i in range(0, rows, piece)]

    looked = []

    def look(*done):
        codes = (asked + local)[len(looked)]
        looked.append(look_up(after(codes, *looked[-1:], *done), codebook))
        return looked[-1]

    block1 = g1.advance()
    up_shard = after(up_weight, block1).reshape(shard_rows, -1, spread, shard_rows)
    up_shard = up_shard.transpose(0, 2, 1, 3).reshape(shard_rows, hidden)
    down_shard = [down_weight[j * shard_rows : (j + 1) * shard_rows] for j in range(spread)]
    beside = jnp.concatenate([output_weight, up_shard, *down_shard], axis=1)
    gathered = lax.all_gather(beside, BOTH, axis=0, tiled=True)
    wide_all = Gathered((gathered,), (width, width + hidden))
    down_all = Gathered((gathered,), (hidden, width), first=width + hidden)
    slots = jnp.concatenate([owner_slot(place), owner_slot(1 - place)])
    block1 = g1.advance(look(beside, slots, g1.order))
    block1 = g1.advance(look(block1))
    g1.advance(look(block1))
    project_all = g1.result()

    normed, q, kv, vec, project_full = project(inputs, project_all)
    kv2 = swap_cores(kv)
    look(q)
    far, near = [swap_cores(f) for f in looked[:2]], looked[2:]
    mixed, mixed_t, logs = attend(lengths, core, after(q, *near), kv, kv2)
    (encoded, grad_resid, mixed_grad), down_pair, up_pair, out_pair, sums = mlp(
        lengths, core, slots, inputs, mixed, cotan, near, far, vec, wide_all, down_all
    )
    grad_down_bias, grad_up_bias, grad_second_gain, grad_second_bias, grad_output_bias = sums
    mlp_sums = Scatter(down_pair, up_pair)

    def back(group, batches, *done, into=()):
        return attend_back(
            lengths,
            core,
            after(q, *done),
            kv,
            kv2,
            mixed_grad,
            mixed_t,
            logs,
            group,
            batches,
            into,
        )

    early = back(GROUPS[0], (0, micro // 2))
    kept = mlp_sums.advance(early[0])
    dq, mine, other = back(GROUPS[0], (micro // 2, micro), kept, into=early)
    came = swap_cores(other)
    pair, partial, small = leave(
        GROUPS[0], core, slots, dq, mine, came, normed, project_full
    )
    first_sums = Scatter(out_pair, pair)
    kept = mlp_sums.advance(*pair)
    dq2, mine2, other2 = back(GROUPS[1], (0, micro), kept)
    came2 = swap_cores(other2)
    rest = [
        jnp.zeros((OUTPUT_BIAS, width), F32),
        grad_output_bias,
        grad_second_gain,
        grad_second_bias,
        grad_down_bias,
        grad_up_bias.reshape(spread, width),
        jnp.zeros((16 - UP_BIAS - spread, width), F32),
    ]
    small = small + jnp.concatenate(rest)
    kept = first_sums.advance(dq2, small), mlp_sums.advance(dq2)
    second_pair, grad_inputs, _ = leave(
        GROUPS[1],
        core,
        slots,
        after(dq2, *kept),
        mine2,
        came2,
        normed,
        project_full,
        partial,
        grad_resid,
        inputs,
        vec,
        small,
    )
    second_sums = Scatter(second_pair)
    sums = (first_sums, second_sums, mlp_sums)
    for _ in range(8):
        for each in sums:
            if not hasattr(each, "total"):
                each.advance(grad_inputs)

    half = width // 2

    def columns(pair, first, count):
        return by_half(*[part[:, first : first + count] for part in pair])

    pair = own_rows(mlp_sums.total)
    grad_down = jnp.concatenate([columns(pair, j * half, half) for j in range(spread)])
    grad_up = columns(pair, spread * half, hidden // 2)
    grad_up = grad_up.reshape(shard_rows, spread, -1, shard_rows).transpose(0, 2, 1, 3)
    grad_up = grad_up.reshape(shard_rows, hidden)
    pair = own_rows(first_sums.total)
    grad_output = columns(pair, 0, half)
    parts = [columns(pair, half, first_sums.total.shape[1] - half)]
    size = second_sums.total.shape[1] - SMALL // 2
    parts.append(by_half(*own_rows(second_sums.total[:, :size])))
    grad_small = second_sums.total[:, size:]
    grad_small = lax.dynamic_slice_in_dim(grad_small, place * shard_rows, shard_rows, axis=0)
    grad_project_weight = jnp.concatenate(
        [
            part[:, i * pairs * 128 : (i + 1) * pairs * 128]
            for i in range(3)
            for (_, pairs), part in zip(GROUPS, parts)
        ],
        axis=1,
    )
    (
        grad_first_gain,
        grad_first_bias,
        grad_query_bias,
        grad_value_bias,
        grad_output_bias,
        grad_second_gain,
        grad_second_bias,
        grad_down_bias,
    ) = grad_small[:, :UP_BIAS].T
    grad_up_bias = grad_small[:, UP_BIAS : UP_BIAS + spread].T.reshape(-1)

    shape = patches.shape
    return (
        encoded.reshape(shape),
        grad_inputs.reshape(shape),
        grad_first_gain,
        grad_first_bias,
        grad_project_weight,
        grad_query_bias,
        grad_value_bias,
        grad_output,
        grad_output_bias,
        grad_second_gain,
        grad_second_bias,
        grad_up,
        grad_up_bias,
        grad_down,
        grad_down_bias,
    )


def solution(mesh):
    split = P(BOTH)
    split_rows = P(BOTH, None)
    patch = P(None, "dp", "seq", None)
    placed = (
        patch,
        P(None, "dp", "seq"),
        P(None, "dp", None),
        patch,
        P("seq", None),
        split,
        split,
        split_rows,
        split,
        split,
        split_rows,
        split,
        split,
        split,
        split_rows,
        split,
        split_rows,
        split,
    )
    return jax.shard_map(
        body,
        mesh=mesh,
        in_specs=placed,
        out_specs=(
            patch,
            patch,
            split,
            split,
            split_rows,
            split,
            split,
            split_rows,
            split,
            split,
            split,
            split_rows,
            split,
            split_rows,
            split,
        ),
        check_vma=False,
    )
```

```python
import functools

import jax
import jax.numpy as jnp
import numpy as np
from jax import lax
from jax.experimental import pallas as pl
from jax.experimental.pallas import tpu as pltpu
from jax.sharding import PartitionSpec as P

HEADS = 12
HEAD_DIM = 64
EPS = 1e-06
COMMIT = 0.5
SCALE = HEAD_DIM ** (-0.5)
NEGATIVE = -1e30
GELU_A = (2 / np.pi) ** 0.5
GELU_B = 0.044715
BOTH = ("dp", "seq")
F32 = jnp.float32
BF16 = jnp.bfloat16
ANY = pl.BlockSpec(memory_space=pl.ANY)
FIRST_GAIN, FIRST_BIAS, QUERY_BIAS, VALUE_BIAS, OUTPUT_BIAS = 0, 1, 2, 3, 4
SECOND_GAIN, SECOND_BIAS, DOWN_BIAS, UP_BIAS = 5, 6, 7, 8
SMALL = 256
GROUPS = ((0, 4), (4, 2))


def params():
    return pltpu.CompilerParams(vmem_limit_bytes=63 << 20)


def cost(micros):
    return pl.CostEstimate(
        flops=int(micros * 0.1e9), bytes_accessed=int(micros * 0.3e6), transcendentals=0
    )


def nn(left, right):
    return jnp.dot(left, right, preferred_element_type=F32)


def nt(left, right):
    return lax.dot_general(left, right, (((1,), (1,)), ((), ())), preferred_element_type=F32)


def tn(left, right):
    return lax.dot_general(left, right, (((0,), (0,)), ((), ())), preferred_element_type=F32)


def stage_masks(chips, core):
    bits = chips.bit_length() - 1
    high = [tuple(1 << b for b in range(at, min(at + 2, bits))) for at in range(2, bits, 2)]
    return high + ([(1,), (2,)] if core == 0 else [(2,), (1,)])


def stage_count():
    return len(stage_masks(lax.axis_size("dp"), 0))


def stage_partners(stage):
    chips = lax.axis_size("dp")
    both = [stage_masks(chips, core)[stage] for core in (0, 1)]
    picks = range(1, 1 << len(both[0]))
    return [tuple(sum(m for i, m in enumerate(masks) if p >> i & 1) for masks in both) for p in picks]


def flat_masks(core):
    return [m for stage in stage_masks(lax.axis_size("dp"), core) for m in stage]


def slot_owner(core):
    slot = jnp.arange(lax.axis_size("dp"), dtype=jnp.int32)
    owners = []
    for own in (0, 1):
        parts = [(slot >> i & 1) * m for i, m in enumerate(flat_masks(own))]
        owners.append(sum(parts) ^ lax.axis_index("dp"))
    return jnp.where(core == 0, owners[0], owners[1]).astype(jnp.int32)


def owner_slot(core):
    apart = jnp.arange(lax.axis_size("dp"), dtype=jnp.int32) ^ lax.axis_index("dp")
    slots = []
    for own in (0, 1):
        slots.append(sum(((apart & m) != 0) * (1 << i) for i, m in enumerate(flat_masks(own))))
    return jnp.where(core == 0, slots[0], slots[1]).astype(jnp.int32)


def swap_cores(block):
    chips = lax.axis_size("dp")
    return lax.ppermute(
        block, BOTH, [(d * 2 + c, d * 2 + 1 - c) for d in range(chips) for c in (0, 1)]
    )


def swap_chips(block, masks):
    chips = lax.axis_size("dp")
    pairs = [(d * 2 + c, (d ^ masks[c]) * 2 + c) for d in range(chips) for c in (0, 1)]
    return lax.ppermute(block, BOTH, pairs)


class Gathered:
    def __init__(self, arrays, shape, order=None, first=0):
        self.arrays, self.shape, self.first = arrays, shape, first
        self.order = jnp.zeros((1,), jnp.int32) if order is None else order

    def specs(self):
        return [ANY] * len(self.arrays)

    def scratch(self):
        return [pltpu.VMEM(self.shape, BF16), pltpu.SemaphoreType.DMA((32,))]

    def copies(self, order_ref, refs, weight, sems):
        copies = []
        if len(refs) == 1:
            rows, width = refs[0].shape[0], weight.shape[1]
            for j in range(weight.shape[0] // rows):
                source = refs[0].at[:, pl.ds(self.first + j * width, width)]
                spot = weight.at[pl.ds(j * rows, rows), :]
                copies.append(pltpu.make_async_copy(source, spot, sems.at[j]))
        else:
            per, rows, half = refs[0].shape
            for b, buf in enumerate(refs):
                for s in range(per):
                    at = b * per + s
                    row = pl.multiple_of(order_ref[at] * rows, 16)
                    col = pl.multiple_of(order_ref[4 * per + b // 2] * half, 128)
                    spot = weight.at[pl.ds(row, rows), pl.ds(col, half)]
                    copies.append(pltpu.make_async_copy(buf.at[s], spot, sems.at[at]))
        return copies


def after(value, *others):
    return lax.optimization_barrier((value, *others))[0]


class Gather:
    def __init__(self, shard):
        self.core = lax.axis_index("seq")
        self.half = shard.shape[1] // 2
        self.mine = lax.dynamic_slice_in_dim(shard, self.core * self.half, self.half, axis=1)
        theirs = lax.dynamic_slice_in_dim(shard, (1 - self.core) * self.half, self.half, axis=1)
        self.came = swap_cores(theirs)
        self.stage = -1
        places = [slot_owner(self.core), slot_owner(1 - self.core)]
        places.append(jnp.stack([self.core, 1 - self.core]).astype(jnp.int32))
        self.order = jnp.concatenate(places)

    def advance(self, *done):
        last = stage_count() - 1
        if self.stage < 0:
            came = after(self.came, *done)
            first, second = (self.mine, came), (came, self.mine)
            first, second = jnp.concatenate(first), jnp.concatenate(second)
            self.block = jnp.where(self.core == 0, first, second)[None]
        elif self.stage < last:
            came = [after(c, *done) for c in self.came]
            self.block = jnp.concatenate([self.block, *came])
        else:
            self.came = after(self.came[0], *done)
            self.high = swap_cores(self.came)
            return self.came
        self.stage += 1
        self.came = [swap_chips(self.block, masks) for masks in stage_partners(self.stage)]
        if self.stage == last:
            self.low = swap_cores(self.block)
        elif self.stage < last - 2:
            return self.advance()
        return self.block

    def result(self):
        chips, rows = 2 * self.block.shape[0], self.block.shape[1]
        shape = (chips * rows, 2 * self.half)
        core, order = self.core, self.order
        if rows % 16 == 0 and self.half % 128 == 0:
            return Gathered((self.block, self.came, self.low, self.high), shape, order)
        place = owner_slot(core), owner_slot(1 - core)
        own = jnp.take(jnp.concatenate([self.block, self.came]), place[0], axis=0)
        other = jnp.take(jnp.concatenate([self.low, self.high]), place[1], axis=0)
        own = own.reshape(chips * rows, self.half)
        other = other.reshape(chips * rows, self.half)
        full = jnp.where(
            core == 0, jnp.concatenate([own, other], 1), jnp.concatenate([other, own], 1)
        )
        return Gathered((full,), shape)


def add_kernel(count, parts, *refs):
    outs = refs[-parts:]
    at = 0
    for i in range(count):
        keep, came = refs[2 * i : 2 * i + 2]
        spot = slice(at, at + keep.shape[3])
        for j, out in enumerate(outs):
            out[:, :, spot] = (keep[j].astype(F32) + came[j].astype(F32)).astype(BF16)
        at += keep.shape[3]


def add_parts(keeps, cames, parts):
    slots, rows, _ = keeps[0].shape
    size = slots // parts
    steps = 2 if size > 1 else 1
    operands, specs = [], []
    for keep, came in zip(keeps, cames):
        width = keep.shape[2]
        operands += [a.reshape(parts, size, rows, width) for a in (keep, came)]
        specs += [pl.BlockSpec((parts, size // steps, rows, width), lambda i: (0, i, 0, 0))] * 2
    total = sum(k.shape[2] for k in keeps)
    out_spec = pl.BlockSpec((size // steps, rows, total), lambda i: (i, 0, 0))
    return pl.pallas_call(
        functools.partial(add_kernel, len(keeps), parts),
        grid=(steps,),
        in_specs=specs,
        out_specs=[out_spec] * parts,
        out_shape=[jax.ShapeDtypeStruct((size, rows, total), BF16)] * parts,
        compiler_params=params(),
        name="add_parts",
        cost_estimate=cost(1 + total * slots * rows * 1.3e-6),
    )(*operands)


class Scatter:
    def __init__(self, *pairs):
        self.keeps = [keep for _, keep in pairs]
        self.cames = [swap_cores(send) for send, _ in pairs]
        self.stage = stage_count()

    def advance(self, *done):
        cames = [after(came, *done) for came in self.cames]
        if self.stage == stage_count() or len(cames) == 1:
            self.stage -= 1
            if self.stage >= 0:
                partners = stage_partners(self.stage)
                keep, *sends = add_parts(self.keeps, cames, 1 + len(partners))
                self.keeps = [keep]
                self.cames = [swap_chips(s, masks) for s, masks in zip(sends, partners)]
                return keep
        total = self.keeps[0].astype(F32)
        for came in cames:
            total = total + came.astype(F32)
        if self.stage > 0:
            self.keeps, self.cames = [total.astype(BF16)], [jnp.zeros_like(total)]
            return self.advance()
        self.total = total[0]
        return self.total


def own_rows(part):
    core = lax.axis_index("seq")
    rows = part.shape[0] // 2
    mine = lax.dynamic_slice_in_dim(part, core * rows, rows, axis=0)
    theirs = lax.dynamic_slice_in_dim(part, (1 - core) * rows, rows, axis=0)
    return mine, swap_cores(theirs)


def by_half(mine, came):
    first = lax.axis_index("seq") == 0
    return jnp.concatenate([jnp.where(first, mine, came), jnp.where(first, came, mine)], axis=1)


def look_kernel(codes_ref, table_ref, *refs):
    out_ref, buf, sems = refs[-3:]
    depth = buf.shape[0]
    table_rows = table_ref.shape[0]
    groups = out_ref.shape[0] // 16

    def start(g):
        slot = lax.rem(g, depth)
        for r in range(16):
            code = codes_ref[g * 16 + r]
            code = jnp.where(code < 0, code + table_rows, code)
            code = jnp.where(code >= table_rows, code - table_rows, code)
            first = lax.shift_left(lax.shift_right_logical(code, 4), 4)
            pltpu.make_async_copy(
                table_ref.at[pl.ds(pl.multiple_of(first, 16), 16), :],
                buf.at[slot, pl.ds(16 * r, 16), :],
                sems.at[slot],
            ).start()

    linear = lax.broadcasted_iota(jnp.int32, (16, 256), 0) * 256 + lax.broadcasted_iota(
        jnp.int32, (16, 256), 1
    )

    def finish(g):
        slot = lax.rem(g, depth)
        pick = jnp.zeros((16, 256), jnp.bool_)
        for r in range(16):
            code = codes_ref[g * 16 + r]
            held = (code >= 0) & (code < table_rows)
            pick = pick | (linear == jnp.where(held, r * 256 + r * 16 + (code & 15), -1))
        pltpu.make_async_copy(buf.at[slot], buf.at[slot], sems.at[slot]).wait()
        rows = nn(pick.astype(F32).astype(BF16), buf[slot])
        out_ref[pl.ds(pl.multiple_of(g * 16, 16), 16), :] = rows.astype(BF16)

    for g in range(depth - 1):
        start(jnp.int32(g))

    def step(g, carry):
        @pl.when(g + depth - 1 < groups)
        def _():
            start(g + depth - 1)

        finish(g)
        return carry

    lax.fori_loop(0, groups, step, 0)


def look_up(codes, table, part, parts, into=()):
    count, width = codes.shape[0], table.shape[1]
    depth = 8
    return pl.pallas_call(
        look_kernel,
        grid_spec=pltpu.PrefetchScalarGridSpec(
            num_scalar_prefetch=1,
            grid=(1,),
            in_specs=[ANY] * (1 + len(into)),
            out_specs=pl.BlockSpec((count, width), lambda i, *_: (part, 0)),
            scratch_shapes=[
                pltpu.VMEM((depth, 256, width), BF16),
                pltpu.SemaphoreType.DMA((depth,)),
            ],
        ),
        out_shape=jax.ShapeDtypeStruct((count * parts, width), BF16),
        input_output_aliases={2 + i: i for i in range(len(into))},
        compiler_params=params(),
        name="look_up",
        cost_estimate=cost(count * 0.0187),
    )(codes, table, *into)


def norm_parts(values):
    mean = jnp.mean(values, axis=-1, keepdims=True)
    centred = values - mean
    spread = jnp.mean(centred * centred, axis=-1, keepdims=True)
    inverse = lax.rsqrt(spread + EPS)
    return centred * inverse, inverse


def norm_back(grad, normed, inverse, gain):
    c = grad * gain
    mean = jnp.mean(c, axis=-1, keepdims=True)
    along = jnp.mean(c * normed, axis=-1, keepdims=True)
    return inverse * (c - mean - normed * along)


def gelu_both(u):
    square = u * u
    t = jnp.tanh(u * (GELU_A + (GELU_A * GELU_B) * square))
    half = 0.5 + 0.5 * t
    slope = half + (0.5 * u) * (1.0 - t * t) * (GELU_A + (3 * GELU_A * GELU_B) * square)
    return u * half, slope


def column_sums(values):
    return jnp.sum(values.astype(F32), axis=0, keepdims=True)


def row_block(tile, columns):
    return pl.BlockSpec((tile, columns), lambda i, *_: (i, 0))


def whole(shape):
    return pl.BlockSpec(shape, lambda i, *_: (0,) * len(shape))


def shaped(dtype, *shape):
    return jax.ShapeDtypeStruct(shape, dtype)


def segment_of(position, lengths_ref, batch):
    end = jnp.int32(0)
    segment = jnp.zeros(position.shape, jnp.int32)
    for s in range(lengths_ref.shape[1]):
        end = end + lengths_ref[batch, s]
        segment = segment + (position >= end).astype(jnp.int32)
    return segment


def fill_mask(mask_ref, lengths_ref, core, batch):
    rows = mask_ref.shape[1]
    query = lax.broadcasted_iota(jnp.int32, (1, rows), 1) + core * rows
    query = segment_of(query, lengths_ref, batch)
    for part, owner in enumerate((core, 1 - core)):
        key = lax.broadcasted_iota(jnp.int32, (rows, 128), 0) + owner * rows
        key = segment_of(key, lengths_ref, batch)
        key = jnp.concatenate([key] * (rows // 128), axis=1)
        mask_ref[part * rows : (part + 1) * rows, :] = jnp.where(key == query, 0.0, NEGATIVE)


def head_lanes(block, head):
    lane = lax.broadcasted_iota(jnp.int32, block.shape, 1)
    return jnp.where((lane < HEAD_DIM) == (head == 0), block, jnp.zeros_like(block))


def attend_kernel(
    lengths_ref, core_ref, q_ref, k_ref, v_ref, k2_ref, v2_ref, o_ref, ot_ref, log_ref, mask_ref
):
    k_ref, v_ref, k2_ref, v2_ref = (ref.at[0] for ref in (k_ref, v_ref, k2_ref, v2_ref))
    fill_mask(mask_ref, lengths_ref, core_ref[0], pl.program_id(0))
    pairs = q_ref.shape[1] // 128

    def scores_of(pair):
        at = slice(pair * 128, pair * 128 + 128)
        k = jnp.concatenate([k_ref[:, at], k2_ref[:, at]], axis=0)
        return [nt(k, head_lanes(q_ref[:, at], head)) + mask_ref[...] for head in range(2)]

    ahead = scores_of(0)
    for pair in range(pairs):
        at = slice(pair * 128, pair * 128 + 128)
        values = jnp.concatenate([v_ref[:, at], v2_ref[:, at]], axis=0).T
        outs, scores = [], ahead
        if pair + 1 < pairs:
            ahead = scores_of(pair + 1)
        for head, score in enumerate(scores):
            peak = jnp.max(score, axis=0, keepdims=True)
            expo = jnp.exp(score - peak)
            total = jnp.sum(expo, axis=0, keepdims=True)
            log_ref[0, pair, head : head + 1, :] = peak + jnp.log(total)
            here = slice(head * HEAD_DIM, head * HEAD_DIM + HEAD_DIM)
            outs.append(nn(values[here], expo.astype(BF16)) * (1.0 / total))
        out = jnp.concatenate(outs, axis=0)
        ot_ref[0, at, :] = out
        o_ref[:, at] = out.T.astype(BF16)


def attend(lengths, core, q, kv, kv2):
    micro = lengths.shape[0]
    rows, width = q.shape[0] // micro, q.shape[1]
    pairs = width // 128
    block = row_block(rows, width)
    keys = pl.BlockSpec((1, rows, width), lambda b, *_: (0, b, 0))
    values = pl.BlockSpec((1, rows, width), lambda b, *_: (1, b, 0))
    area = micro * HEADS * rows * 2 * rows
    return pl.pallas_call(
        attend_kernel,
        grid_spec=pltpu.PrefetchScalarGridSpec(
            num_scalar_prefetch=2,
            grid=(micro,),
            in_specs=[block, keys, values, keys, values],
            out_specs=[
                block,
                pl.BlockSpec((1, width, rows), lambda b, *_: (b, 0, 0)),
                pl.BlockSpec((1, pairs, 2, rows), lambda b, *_: (b, 0, 0, 0)),
            ],
            scratch_shapes=[pltpu.VMEM((2 * rows, rows), F32)],
        ),
        out_shape=[
            shaped(BF16, *q.shape),
            shaped(F32, micro, width, rows),
            shaped(F32, micro, pairs, 2, rows),
        ],
        compiler_params=params(),
        name="attend",
        cost_estimate=cost(17),
    )(lengths, core, q, kv, kv, kv2, kv2)


def attend_back_kernel(
    first_batch,
    lengths_ref,
    core_ref,
    q_ref,
    k_ref,
    v_ref,
    k2_ref,
    v2_ref,
    g_ref,
    ot_ref,
    log_ref,
    *refs,
):
    dq_ref, mine_ref, other_ref, mask_ref = refs[-4:]
    rows = q_ref.shape[0]
    k_ref, v_ref, k2_ref, v2_ref = (ref.at[0] for ref in (k_ref, v_ref, k2_ref, v2_ref))
    fill_mask(mask_ref, lengths_ref, core_ref[0], pl.program_id(0) + first_batch)
    for pair in range(q_ref.shape[1] // 128):
        at = slice(pair * 128, pair * 128 + 128)
        q = q_ref[:, at]
        g = g_ref[:, at]
        k = jnp.concatenate([k_ref[:, at], k2_ref[:, at]], axis=0)
        v = jnp.concatenate([v_ref[:, at], v2_ref[:, at]], axis=0)
        keys = k.T
        products = g.astype(F32).T * ot_ref[0, at, :]
        dq, dk, dv = [], 0.0, 0.0
        for head in range(2):
            here = slice(head * HEAD_DIM, head * HEAD_DIM + HEAD_DIM)
            q_head, g_head = head_lanes(q, head), head_lanes(g, head)
            p = jnp.exp(nt(k, q_head) + (mask_ref[...] - log_ref[0, pair, head : head + 1, :]))
            inner = jnp.sum(products[here], axis=0, keepdims=True)
            ds = (p * (nt(v, g_head) - inner)).astype(BF16)
            dq.append(nn(keys[here], ds))
            dk = dk + nn(ds, q_head)
            dv = dv + nn(p.astype(BF16), g_head)
        dq_ref[:, at] = (jnp.concatenate(dq, axis=0).T * SCALE).astype(BF16)
        for i, grad in enumerate((dk, dv)):
            mine_ref[i, :, at] = grad[:rows].astype(BF16)
            other_ref[i, :, at] = grad[rows:].astype(BF16)


def attend_back(lengths, core, q, kv, kv2, g, ot, logs, group, batches, into=()):
    micro = lengths.shape[0]
    rows = q.shape[0] // micro
    first, pairs = group
    width = pairs * 128
    at = first // pairs
    start, stop = batches
    block = pl.BlockSpec((rows, width), lambda b, *_: (b + start, at))
    keys = pl.BlockSpec((1, rows, width), lambda b, *_: (0, b + start, at))
    values = pl.BlockSpec((1, rows, width), lambda b, *_: (1, b + start, at))
    both = pl.BlockSpec((2, rows, width), lambda b, *_: (0, b + start, 0))
    count = micro * rows
    operands = (lengths, core, q, kv, kv, kv2, kv2, g, ot, logs)
    return pl.pallas_call(
        functools.partial(attend_back_kernel, start),
        grid_spec=pltpu.PrefetchScalarGridSpec(
            num_scalar_prefetch=2,
            grid=(stop - start,),
            in_specs=[
                block,
                keys,
                values,
                keys,
                values,
                block,
                pl.BlockSpec((1, width, rows), lambda b, *_: (b + start, at, 0)),
                pl.BlockSpec((1, pairs, 2, rows), lambda b, *_: (b + start, at, 0, 0)),
            ]
            + [ANY] * len(into),
            out_specs=[pl.BlockSpec((rows, width), lambda b, *_: (b + start, 0)), both, both],
            scratch_shapes=[pltpu.VMEM((2 * rows, rows), F32)],
        ),
        out_shape=[shaped(BF16, count, width)] + [shaped(BF16, 2, count, width)] * 2,
        input_output_aliases={len(operands) + i: i for i in range(len(into))},
        compiler_params=params(),
        name="attend_back",
        cost_estimate=cost(1.2 * pairs * (stop - start)),
    )(*operands, *into)


def project_kernel(weight_in, order_ref, x_ref, *refs):
    *sources, h_ref, q_ref, kv_ref, vec_ref, full_ref, weight, sems, full_sem = refs
    width = x_ref.shape[1]
    i = pl.program_id(0)
    full_copy = pltpu.make_async_copy(weight, full_ref, full_sem)

    @pl.when(i == 0)
    def _():
        copies = weight_in.copies(order_ref, sources, weight, sems)
        for copy in copies:
            copy.start()
        for copy in copies:
            copy.wait()
        full_copy.start()
        small = weight[:, 3 * width : 3 * width + 128].astype(F32).T
        vec_ref[...] = small[: vec_ref.shape[0]]

    vec = lambda i: vec_ref[i : i + 1, :]
    normed, _ = norm_parts(x_ref[...].astype(F32))
    h = (normed * vec(FIRST_GAIN) + vec(FIRST_BIAS)).astype(BF16)
    h_ref[...] = h
    q = (nn(h, weight[:, :width]) + vec(QUERY_BIAS)).astype(BF16)
    q_ref[...] = (q.astype(F32) * SCALE).astype(BF16)
    kv_ref[0] = nn(h, weight[:, width : 2 * width]).astype(BF16)
    values = nn(h, weight[:, 2 * width : 3 * width]) + vec(VALUE_BIAS)
    kv_ref[1] = values.astype(BF16)

    @pl.when(i == pl.num_programs(0) - 1)
    def _():
        full_copy.wait()


def project(x, weight):
    rows, width = x.shape
    tile = 256
    block = row_block(tile, width)
    return pl.pallas_call(
        functools.partial(project_kernel, weight),
        grid_spec=pltpu.PrefetchScalarGridSpec(
            num_scalar_prefetch=1,
            grid=(rows // tile,),
            in_specs=[block] + weight.specs(),
            out_specs=[
                block,
                block,
                pl.BlockSpec((2, tile, width), lambda i, *_: (0, i, 0)),
                whole((16, width)),
                ANY,
            ],
            scratch_shapes=weight.scratch() + [pltpu.SemaphoreType.DMA],
        ),
        out_shape=[
            shaped(BF16, rows, width),
            shaped(BF16, rows, width),
            shaped(BF16, 2, rows, width),
            shaped(F32, 16, width),
            shaped(BF16, *weight.shape),
        ],
        compiler_params=params(),
        name="project",
        cost_estimate=cost(10),
    )(weight.order, x, *weight.arrays)


def store_rows(ref, slot_ref, first, value, at=0):
    value = value.astype(BF16)
    columns = slice(at, at + value.shape[1])
    if len(ref.shape) == 2:
        ref[:, columns] = value
        return
    chips, rows, _ = ref.shape
    for chip in range(chips):
        ref[slot_ref[first + chip], :, columns] = value[chip * rows : chip * rows + rows]


def by_slots(chips, rows):
    return rows // chips % 16 == 0


def in_slots(product, slots):
    chips = slots.shape[0]
    if product.ndim == 3:
        return product
    product = product.reshape(chips, -1, product.shape[1])
    return jnp.zeros_like(product).at[slots].set(product)


def pair_in_slots(slots, send, keep):
    chips = slots.shape[0] // 2
    return in_slots(send, slots[chips:]), in_slots(keep, slots[:chips])


def product_shape(chips, rows, columns):
    if by_slots(chips, rows):
        return (chips, rows // chips, columns)
    return (rows, columns)


def product_spec(chips, rows, columns, index):
    lead = (0, 0) if by_slots(chips, rows) else (0,)
    return pl.BlockSpec(
        product_shape(chips, rows, columns), lambda i, *_: lead + (index(i),)
    )


def mlp_kernel(
    streams,
    wide_in,
    down_in,
    lengths_ref,
    core_ref,
    slot_ref,
    x_ref,
    o_ref,
    cot_ref,
    near_ref,
    far_ref,
    vec_ref,
    source_ref,
    enc_ref,
    d_ref,
    go_ref,
    down_send_ref,
    down_keep_ref,
    up_send_ref,
    up_keep_ref,
    out_send_ref,
    out_keep_ref,
    db_ref,
    ub_ref,
    gain_ref,
    bias_ref,
    ob_ref,
    wide,
    down,
    active_all,
    upper_all,
    normed_all,
    z_all,
    low_all,
    slope_tile,
    wide_sems,
    down_sems,
):
    i = pl.program_id(0)
    steps = pl.num_programs(0) - active_all.shape[0]
    tiles = lengths_ref.shape[0]
    width = x_ref.shape[1]
    rows = o_ref.shape[0] // tiles
    blocks = active_all.shape[0]
    core = core_ref[0]
    chips = slot_ref.shape[0] // 2
    copies = wide_in.copies(None, [source_ref], wide, wide_sems)
    copies += down_in.copies(None, [source_ref], down, down_sems)

    @pl.when(i == 0)
    def _():
        for copy in copies:
            copy.start()
        for ref in (db_ref, ub_ref, gain_ref, bias_ref, ob_ref):
            ref[...] = jnp.zeros(ref.shape, F32)
        for copy in copies:
            copy.wait()

    def up_columns(b):
        return wide[:, width * (b + 1) : width * (b + 2)]

    def down_rows(b):
        return down[width * b : width * (b + 1), :]

    def stream(k):
        tile = i * streams + k
        here = slice(k * rows, k * rows + rows)
        at = pl.ds(pl.multiple_of(tile * rows, rows), rows)
        vec = lambda k: vec_ref[k : k + 1, :]
        r = x_ref[here, :].astype(F32) + nn(o_ref[at, :], wide[:, :width]) + vec(OUTPUT_BIAS)
        yield
        normed, inverse = norm_parts(r)
        h = (normed * vec(SECOND_GAIN) + vec(SECOND_BIAS)).astype(BF16)
        normed_all[at, :] = h
        yield

        def rise(b):
            return nn(h, up_columns(b)) + vec(UP_BIAS + b)

        upper = rise(0)
        for b in range(blocks):
            now = upper
            if b + 1 < blocks:
                upper = rise(b + 1)
            active, slope = gelu_both(now)
            active_all[b, at, :] = active.astype(BF16)
            slope_tile[k * blocks + b] = slope.astype(BF16)
            yield
        filled = lengths_ref[tile, 0]
        for j in range(1, lengths_ref.shape[1]):
            filled = filled + lengths_ref[tile, j]
        position = lax.broadcasted_iota(jnp.int32, (rows, 1), 0) + core * rows
        live = (position < filled).astype(F32)
        z = r + vec(DOWN_BIAS)
        for b in range(blocks):
            z = z + nn(active_all[b, at, :], down_rows(b))
        yield
        enc_ref[here, :] = (live * z).astype(BF16)
        near, far = near_ref[here, :].astype(F32), far_ref[here, :].astype(F32)
        gz = live * (cot_ref[here, :].astype(F32) + COMMIT * (z - (near + far)))
        low = gz.astype(BF16)
        z_all[at, :] = low
        db_ref[...] += column_sums(low)
        yield
        e = 0.0
        fall = nt(low, down_rows(0))
        for b in range(blocks):
            now = fall
            if b + 1 < blocks:
                fall = nt(low, down_rows(b + 1))
            gu = (now * slope_tile[k * blocks + b].astype(F32)).astype(BF16)
            upper_all[b, at, :] = gu
            ub_ref[:, width * b : width * (b + 1)] += column_sums(gu)
            e = e + nt(gu, up_columns(b))
            yield
        gain_ref[...] += column_sums(e * normed)
        bias_ref[...] += column_sums(e)
        d = gz + norm_back(e, normed, inverse, vec(SECOND_GAIN))
        d_ref[here, :] = d
        low = d.astype(BF16)
        low_all[at, :] = low
        ob_ref[...] += column_sums(low)
        yield
        go_ref[here, :] = nt(low, wide[:, :width]).astype(BF16)

    @pl.when(i < steps)
    def _():
        running = [stream(k) for k in range(streams)]
        while running:
            running = [each for each in running if next(each, "end") != "end"]

    def split(out, send_ref, keep_ref):
        half = out.shape[1] // 2
        first = core == 0
        store_rows(keep_ref, slot_ref, 0, jnp.where(first, out[:, :half], out[:, half:]))
        store_rows(send_ref, slot_ref, chips, jnp.where(first, out[:, half:], out[:, :half]))

    for j in range(blocks):

        @pl.when(i == steps + j)
        def _():
            split(tn(active_all[j], z_all[...]), down_send_ref, down_keep_ref)
            column = lax.rem(j + blocks // 2 * (1 - core), blocks)
            product = tn(normed_all[...], upper_all[column])
            if j < blocks // 2:
                store_rows(up_send_ref, slot_ref, chips, product)
            else:
                store_rows(up_keep_ref, slot_ref, 0, product)
            if j == blocks - 1:
                split(tn(o_ref[...], low_all[...]), out_send_ref, out_keep_ref)


def mlp(lengths, core, slots, x, o, cot, near, far, vec, wide, down):
    rows, width = x.shape
    hidden = down.shape[0]
    tiles, blocks = lengths.shape[0], hidden // width
    tile = rows // tiles
    streams = 1
    steps = tiles // streams
    chips = slots.shape[0] // 2
    block = pl.BlockSpec(
        (streams * tile, width), lambda i, *_: (jnp.minimum(i, steps - 1), 0)
    )
    row, long_row = whole((1, width)), whole((1, hidden))
    down_spec = product_spec(chips, width, width // 2, lambda i: jnp.maximum(i - steps, 0))
    send_spec = product_spec(chips, width, width, lambda i: jnp.clip(i - steps, 0, blocks // 2 - 1))
    keep_spec = product_spec(chips, width, width, lambda i: jnp.maximum(i - steps - blocks // 2, 0))
    out_spec = product_spec(chips, width, width // 2, lambda i: 0)
    half_hidden = shaped(BF16, *product_shape(chips, width, hidden // 2))
    half_width = shaped(BF16, *product_shape(chips, width, width // 2))
    results = pl.pallas_call(
        functools.partial(mlp_kernel, streams, wide, down),
        grid_spec=pltpu.PrefetchScalarGridSpec(
            num_scalar_prefetch=3,
            grid=(steps + blocks,),
            in_specs=[block, whole(o.shape), block, block, block]
            + [whole(vec.shape), ANY],
            out_specs=[block, block, block]
            + [down_spec, down_spec, send_spec, keep_spec, out_spec, out_spec]
            + [row, long_row, row, row, row],
            scratch_shapes=[
                pltpu.VMEM(wide.shape, BF16),
                pltpu.VMEM(down.shape, BF16),
                pltpu.VMEM((blocks, rows, width), BF16),
                pltpu.VMEM((blocks, rows, width), BF16),
                pltpu.VMEM((rows, width), BF16),
                pltpu.VMEM((rows, width), BF16),
                pltpu.VMEM((rows, width), BF16),
                pltpu.VMEM((streams * blocks, tile, width), BF16),
                pltpu.SemaphoreType.DMA((blocks,)),
                pltpu.SemaphoreType.DMA((blocks,)),
            ],
        ),
        out_shape=[
            shaped(BF16, rows, width),
            shaped(F32, rows, width),
            shaped(BF16, rows, width),
            half_hidden,
            half_hidden,
            half_hidden,
            half_hidden,
            half_width,
            half_width,
            shaped(F32, 1, width),
            shaped(F32, 1, hidden),
            shaped(F32, 1, width),
            shaped(F32, 1, width),
            shaped(F32, 1, width),
        ],
        compiler_params=params(),
        name="mlp",
        cost_estimate=cost(55),
    )(lengths, core, slots, x, o, cot, near, far, vec, *wide.arrays)
    down_pair, up_pair, out_pair = (pair_in_slots(slots, *results[k : k + 2]) for k in (3, 5, 7))
    return results[:3], down_pair, up_pair, out_pair, results[9:]


def leave_kernel(group, last, core_ref, slot_ref, *refs):
    refs = list(refs)
    take = lambda count: [refs.pop(0) for _ in range(count)]
    dq_ref, mine_ref, came_ref, h_ref, full_ref = take(5)
    if last:
        e_in_ref, d_ref, x_ref, vec_ref, small_ref = take(5)
        send_ref, keep_ref, dx_ref = take(3)
        sums = take(1)[0]
    else:
        send_ref, keep_ref, e_ref, sums = take(4)
    weight, grads, sems = refs
    first, pairs = group
    size = pairs * 128
    i = pl.program_id(0)
    rows = dq_ref.shape[0]
    width = h_ref.shape[1]
    core = core_ref[0]
    chips = slot_ref.shape[0] // 2
    copies = []
    for part in range(3):
        source = full_ref.at[:, pl.ds(part * width + first * 128, size)]
        spot = weight.at[:, pl.ds(part * size, size)]
        copies.append(pltpu.make_async_copy(source, spot, sems.at[part]))

    @pl.when(i == 0)
    def _():
        for copy in copies:
            copy.start()
        for copy in copies:
            copy.wait()
        sums[...] = jnp.zeros(sums.shape, F32)

    @pl.when(i < pl.num_programs(0) - 1)
    def _():
        at = pl.ds(pl.multiple_of(i * rows, rows), rows)
        here = slice(first * 128, first * 128 + size)
        dq = dq_ref[...]
        parts = [dq]
        for k in range(2):
            total = mine_ref[k].astype(F32) + came_ref[k].astype(F32)
            parts.append(total.astype(BF16))
        sums[QUERY_BIAS : QUERY_BIAS + 1, here] += column_sums(dq)
        sums[VALUE_BIAS : VALUE_BIAS + 1, here] += column_sums(parts[2])
        grad = jnp.concatenate(parts, axis=1)
        half = grad.shape[1] // 2
        grads[0, at, :] = grad[:, :half]
        grads[1, at, :] = grad[:, half:]
        e = nt(grad, weight[...])
        if last:
            e = e + e_in_ref[...]
            normed, inverse = norm_parts(x_ref[...].astype(F32))
            sums[FIRST_GAIN : FIRST_GAIN + 1, :] += column_sums(e * normed)
            sums[FIRST_BIAS : FIRST_BIAS + 1, :] += column_sums(e)
            back = norm_back(e, normed, inverse, vec_ref[FIRST_GAIN : FIRST_GAIN + 1, :])
            dx_ref[...] = (d_ref[...] + back).astype(BF16)
        else:
            e_ref[...] = e

    @pl.when(i == pl.num_programs(0) - 1)
    def _():
        store_rows(send_ref, slot_ref, chips, tn(h_ref[...], grads[1 - core]))
        store_rows(keep_ref, slot_ref, 0, tn(h_ref[...], grads[core]))
        if last:
            small = sums[...] + small_ref[...]
            small = jnp.concatenate([small, jnp.zeros((SMALL // 2 - 16, width), F32)]).T
            store_rows(send_ref, slot_ref, chips, small, grads.shape[2])
            store_rows(keep_ref, slot_ref, 0, small, grads.shape[2])


def leave(group, core, slots, dq, mine, came, h, full, *rest):
    rows, width = h.shape
    size = dq.shape[1]
    last = bool(rest)
    tile = 256
    tiles = rows // tile
    chips = slots.shape[0] // 2
    half = 3 * size // 2
    columns = half + (SMALL // 2 if last else 0)

    def part(columns):
        return pl.BlockSpec((tile, columns), lambda i, *_: (jnp.minimum(i, tiles - 1), 0))

    both = pl.BlockSpec((2, tile, size), lambda i, *_: (0, jnp.minimum(i, tiles - 1), 0))
    block = part(width)
    in_specs = [part(size), both, both, whole(h.shape), ANY]
    if last:
        in_specs += [block, block, block, whole(rest[3].shape), whole(rest[4].shape)]
    product = product_spec(chips, width, columns, lambda i: 0)
    product_out = shaped(BF16, *product_shape(chips, width, columns))
    send, keep, out, sums = pl.pallas_call(
        functools.partial(leave_kernel, group, last),
        grid_spec=pltpu.PrefetchScalarGridSpec(
            num_scalar_prefetch=2,
            grid=(tiles + 1,),
            in_specs=in_specs,
            out_specs=[product, product, block, whole((16, width))],
            scratch_shapes=[
                pltpu.VMEM((width, 3 * size), BF16),
                pltpu.VMEM((2, rows, half), BF16),
                pltpu.SemaphoreType.DMA((3,)),
            ],
        ),
        out_shape=[
            product_out,
            product_out,
            shaped(BF16 if last else F32, rows, width),
            shaped(F32, 16, width),
        ],
        compiler_params=params(),
        name="leave",
        cost_estimate=cost(13),
    )(core, slots, dq, mine, came, h, full, *rest)
    return pair_in_slots(slots, send, keep), out, sums


def body(
    patches,
    code_index,
    lengths,
    cotangent,
    codebook,
    first_gain,
    first_bias,
    project_weight,
    query_bias,
    value_bias,
    output_weight,
    output_bias,
    second_gain,
    second_bias,
    up_weight,
    up_bias,
    down_weight,
    down_bias,
):
    micro, _, local_rows, width = patches.shape
    rows = micro * local_rows
    hidden = up_weight.shape[1]
    place = lax.axis_index("seq")
    core = place.reshape(1).astype(jnp.int32)
    lengths = lengths[:, 0]
    shard_rows = project_weight.shape[0]
    spread = hidden // width

    small = [
        first_gain,
        first_bias,
        query_bias,
        value_bias,
        output_bias,
        second_gain,
        second_bias,
        down_bias,
    ]
    small += [up_bias[j * shard_rows : (j + 1) * shard_rows] for j in range(spread)]
    line = lax.broadcasted_iota(jnp.int32, (16, shard_rows), 0)
    table = jnp.zeros((16, shard_rows), BF16)
    for j, vector in enumerate(small):
        table = jnp.where(line == j, vector[None, :], table)
    small = jnp.pad(table.T, ((0, 0), (0, SMALL - 16)))
    g1 = Gather(jnp.concatenate([project_weight, small], axis=1))
    inputs = patches.reshape(rows, width)
    cotan = cotangent.reshape(rows, width)
    codes = code_index.reshape(-1)
    local = codes - place * codebook.shape[0]
    asked = swap_cores(codes) - place * codebook.shape[0]
    piece = rows // 2
    asked = [asked[i : i + piece] for i in range(0, rows, piece)]
    local = [local[i : i + piece] for i in range(0, rows, piece)]

    looked = []

    def look(*done):
        at = len(looked)
        codes = after((asked + local)[at], *looked[-1:], *done)
        into = looked[-1:] if at % 2 else ()
        looked.append(look_up(codes, codebook, at % 2, 2, into))
        return looked[-1]

    block1 = g1.advance()
    up_shard = after(up_weight, block1).reshape(shard_rows, -1, spread, shard_rows)
    up_shard = up_shard.transpose(0, 2, 1, 3).reshape(shard_rows, hidden)
    down_shard = [down_weight[j * shard_rows : (j + 1) * shard_rows] for j in range(spread)]
    beside = jnp.concatenate([output_weight, up_shard, *down_shard], axis=1)
    gathered = lax.all_gather(beside, BOTH, axis=0, tiled=True)
    wide_all = Gathered((gathered,), (width, width + hidden))
    down_all = Gathered((gathered,), (hidden, width), first=width + hidden)
    slots = jnp.concatenate([owner_slot(place), owner_slot(1 - place)])
    block1 = g1.advance(look(beside, slots, g1.order))
    block1 = g1.advance(look(block1))
    g1.advance(look(block1))
    project_all = g1.result()

    normed, q, kv, vec, project_full = project(inputs, project_all)
    kv2 = swap_cores(kv)
    look(q)
    far, near = swap_cores(looked[1]), looked[3]
    mixed, mixed_t, logs = attend(lengths, core, after(q, near), kv, kv2)
    (encoded, grad_resid, mixed_grad), down_pair, up_pair, out_pair, sums = mlp(
        lengths, core, slots, inputs, mixed, cotan, near, far, vec, wide_all, down_all
    )
    grad_down_bias, grad_up_bias, grad_second_gain, grad_second_bias, grad_output_bias = sums
    mlp_sums = Scatter(down_pair, up_pair)

    def back(group, batches, *done, into=()):
        return attend_back(
            lengths,
            core,
            after(q, *done),
            kv,
            kv2,
            mixed_grad,
            mixed_t,
            logs,
            group,
            batches,
            into,
        )

    early = back(GROUPS[0], (0, micro // 2))
    kept = mlp_sums.advance(early[0])
    dq, mine, other = back(GROUPS[0], (micro // 2, micro), kept, into=early)
    came = swap_cores(other)
    pair, partial, small = leave(
        GROUPS[0], core, slots, dq, mine, came, normed, project_full
    )
    kept = mlp_sums.advance(*pair)
    first_sums = Scatter(*[(after(send, kept), keep) for send, keep in (out_pair, pair)])
    early = back(GROUPS[1], (0, micro // 2), kept)
    kept = first_sums.advance(early[0])
    dq2, mine2, other2 = back(GROUPS[1], (micro // 2, micro), kept, into=early)
    came2 = swap_cores(other2)
    rest = [
        jnp.zeros((OUTPUT_BIAS, width), F32),
        grad_output_bias,
        grad_second_gain,
        grad_second_bias,
        grad_down_bias,
        grad_up_bias.reshape(spread, width),
        jnp.zeros((16 - UP_BIAS - spread, width), F32),
    ]
    small = small + jnp.concatenate(rest)
    kept = mlp_sums.advance(dq2)
    kept = first_sums.advance(kept, small)
    second_pair, grad_inputs, _ = leave(
        GROUPS[1],
        core,
        slots,
        after(dq2, kept),
        mine2,
        came2,
        normed,
        project_full,
        partial,
        grad_resid,
        inputs,
        vec,
        small,
    )
    second_sums = Scatter(second_pair)

    def finish(sums, kept):
        while not hasattr(sums, "total"):
            kept = sums.advance(kept)
        return kept

    half = width // 2

    def columns(pair, first, count):
        return by_half(*[part[:, first : first + count] for part in pair])

    kept = finish(mlp_sums, grad_inputs)
    kept = second_sums.advance(kept)
    kept = first_sums.advance(kept)
    kept = second_sums.advance(kept)
    pair = own_rows(after(mlp_sums.total, kept))
    grad_down = jnp.concatenate([columns(pair, j * half, half) for j in range(spread)])
    grad_up = columns(pair, spread * half, hidden // 2)
    grad_up = grad_up.reshape(shard_rows, spread, -1, shard_rows).transpose(0, 2, 1, 3)
    grad_up = grad_up.reshape(shard_rows, hidden)
    kept = finish(first_sums, after(kept, grad_up, grad_down))
    kept = second_sums.advance(kept)
    finish(second_sums, kept)
    pair = own_rows(first_sums.total)
    grad_output = columns(pair, 0, half)
    parts = [columns(pair, half, first_sums.total.shape[1] - half)]
    size = second_sums.total.shape[1] - SMALL // 2
    parts.append(by_half(*own_rows(second_sums.total[:, :size])))
    grad_small = second_sums.total[:, size:]
    grad_small = lax.dynamic_slice_in_dim(grad_small, place * shard_rows, shard_rows, axis=0)
    grad_project_weight = jnp.concatenate(
        [
            part[:, i * pairs * 128 : (i + 1) * pairs * 128]
            for i in range(3)
            for (_, pairs), part in zip(GROUPS, parts)
        ],
        axis=1,
    )
    (
        grad_first_gain,
        grad_first_bias,
        grad_query_bias,
        grad_value_bias,
        grad_output_bias,
        grad_second_gain,
        grad_second_bias,
        grad_down_bias,
    ) = grad_small[:, :UP_BIAS].T
    grad_up_bias = grad_small[:, UP_BIAS : UP_BIAS + spread].T.reshape(-1)

    shape = patches.shape
    return (
        encoded.reshape(shape),
        grad_inputs.reshape(shape),
        grad_first_gain,
        grad_first_bias,
        grad_project_weight,
        grad_query_bias,
        grad_value_bias,
        grad_output,
        grad_output_bias,
        grad_second_gain,
        grad_second_bias,
        grad_up,
        grad_up_bias,
        grad_down,
        grad_down_bias,
    )


def solution(mesh):
    split = P(BOTH)
    split_rows = P(BOTH, None)
    patch = P(None, "dp", "seq", None)
    placed = (
        patch,
        P(None, "dp", "seq"),
        P(None, "dp", None),
        patch,
        P("seq", None),
        split,
        split,
        split_rows,
        split,
        split,
        split_rows,
        split,
        split,
        split,
        split_rows,
        split,
        split_rows,
        split,
    )
    return jax.shard_map(
        body,
        mesh=mesh,
        in_specs=placed,
        out_specs=(
            patch,
            patch,
            split,
            split,
            split_rows,
            split,
            split,
            split_rows,
            split,
            split,
            split,
            split_rows,
            split,
            split_rows,
            split,
        ),
        check_vma=False,
    )
```

```python
import functools

import jax
import jax.numpy as jnp
import numpy as np
from jax import lax
from jax.experimental import pallas as pl
from jax.experimental.pallas import tpu as pltpu
from jax.sharding import PartitionSpec as P

HEADS = 12
HEAD_DIM = 64
EPS = 1e-06
COMMIT = 0.5
SCALE = HEAD_DIM ** (-0.5)
NEGATIVE = -1e30
GELU_A = (2 / np.pi) ** 0.5
GELU_B = 0.044715
BOTH = ("dp", "seq")
F32 = jnp.float32
BF16 = jnp.bfloat16
ANY = pl.BlockSpec(memory_space=pl.ANY)
FIRST_GAIN, FIRST_BIAS, QUERY_BIAS, VALUE_BIAS, OUTPUT_BIAS = 0, 1, 2, 3, 4
SECOND_GAIN, SECOND_BIAS, DOWN_BIAS, UP_BIAS = 5, 6, 7, 8
SMALL = 256
GROUPS = ((0, 4), (4, 2))


def params():
    return pltpu.CompilerParams(vmem_limit_bytes=63 << 20)


def cost(micros):
    return pl.CostEstimate(
        flops=int(micros * 0.1e9), bytes_accessed=int(micros * 0.3e6), transcendentals=0
    )


def nn(left, right):
    return jnp.dot(left, right, preferred_element_type=F32)


def nt(left, right):
    return lax.dot_general(left, right, (((1,), (1,)), ((), ())), preferred_element_type=F32)


def tn(left, right):
    return lax.dot_general(left, right, (((0,), (0,)), ((), ())), preferred_element_type=F32)


def stage_masks(chips, core):
    bits = chips.bit_length() - 1
    high = [tuple(1 << b for b in range(at, min(at + 2, bits))) for at in range(2, bits, 2)]
    return high + ([(1,), (2,)] if core == 0 else [(2,), (1,)])


def stage_count():
    return len(stage_masks(lax.axis_size("dp"), 0))


def stage_partners(stage):
    chips = lax.axis_size("dp")
    both = [stage_masks(chips, core)[stage] for core in (0, 1)]
    picks = range(1, 1 << len(both[0]))
    return [tuple(sum(m for i, m in enumerate(masks) if p >> i & 1) for masks in both) for p in picks]


def flat_masks(core):
    return [m for stage in stage_masks(lax.axis_size("dp"), core) for m in stage]


def slot_owner(core):
    slot = jnp.arange(lax.axis_size("dp"), dtype=jnp.int32)
    owners = []
    for own in (0, 1):
        parts = [(slot >> i & 1) * m for i, m in enumerate(flat_masks(own))]
        owners.append(sum(parts) ^ lax.axis_index("dp"))
    return jnp.where(core == 0, owners[0], owners[1]).astype(jnp.int32)


def owner_slot(core):
    apart = jnp.arange(lax.axis_size("dp"), dtype=jnp.int32) ^ lax.axis_index("dp")
    slots = []
    for own in (0, 1):
        slots.append(sum(((apart & m) != 0) * (1 << i) for i, m in enumerate(flat_masks(own))))
    return jnp.where(core == 0, slots[0], slots[1]).astype(jnp.int32)


def swap_cores(block):
    chips = lax.axis_size("dp")
    return lax.ppermute(
        block, BOTH, [(d * 2 + c, d * 2 + 1 - c) for d in range(chips) for c in (0, 1)]
    )


def swap_chips(block, masks):
    chips = lax.axis_size("dp")
    pairs = [(d * 2 + c, (d ^ masks[c]) * 2 + c) for d in range(chips) for c in (0, 1)]
    return lax.ppermute(block, BOTH, pairs)


class Gathered:
    def __init__(self, arrays, shape, order=None, first=0):
        self.arrays, self.shape, self.first = arrays, shape, first
        self.order = jnp.zeros((1,), jnp.int32) if order is None else order

    def specs(self):
        return [ANY] * len(self.arrays)

    def scratch(self):
        return [pltpu.VMEM(self.shape, BF16), pltpu.SemaphoreType.DMA((32,))]

    def copies(self, order_ref, refs, weight, sems):
        copies = []
        if len(refs) == 1:
            rows, width = refs[0].shape[0], weight.shape[1]
            for j in range(weight.shape[0] // rows):
                source = refs[0].at[:, pl.ds(self.first + j * width, width)]
                spot = weight.at[pl.ds(j * rows, rows), :]
                copies.append(pltpu.make_async_copy(source, spot, sems.at[j]))
        else:
            per, rows, half = refs[0].shape
            for b, buf in enumerate(refs):
                for s in range(per):
                    at = b * per + s
                    row = pl.multiple_of(order_ref[at] * rows, 16)
                    col = pl.multiple_of(order_ref[4 * per + b // 2] * half, 128)
                    spot = weight.at[pl.ds(row, rows), pl.ds(col, half)]
                    copies.append(pltpu.make_async_copy(buf.at[s], spot, sems.at[at]))
        return copies


def after(value, *others):
    return lax.optimization_barrier((value, *others))[0]


class Gather:
    def __init__(self, shard):
        self.core = lax.axis_index("seq")
        self.half = shard.shape[1] // 2
        self.mine = lax.dynamic_slice_in_dim(shard, self.core * self.half, self.half, axis=1)
        theirs = lax.dynamic_slice_in_dim(shard, (1 - self.core) * self.half, self.half, axis=1)
        self.came = swap_cores(theirs)
        self.stage = -1
        places = [slot_owner(self.core), slot_owner(1 - self.core)]
        places.append(jnp.stack([self.core, 1 - self.core]).astype(jnp.int32))
        self.order = jnp.concatenate(places)

    def advance(self, *done):
        last = stage_count() - 1
        if self.stage < 0:
            came = after(self.came, *done)
            first, second = (self.mine, came), (came, self.mine)
            first, second = jnp.concatenate(first), jnp.concatenate(second)
            self.block = jnp.where(self.core == 0, first, second)[None]
        elif self.stage < last:
            came = [after(c, *done) for c in self.came]
            self.block = jnp.concatenate([self.block, *came])
        else:
            self.came = after(self.came[0], *done)
            self.high = swap_cores(self.came)
            return self.came
        self.stage += 1
        self.came = [swap_chips(self.block, masks) for masks in stage_partners(self.stage)]
        if self.stage == last:
            self.low = swap_cores(self.block)
        elif self.stage < last - 2:
            return self.advance()
        return self.block

    def result(self):
        chips, rows = 2 * self.block.shape[0], self.block.shape[1]
        shape = (chips * rows, 2 * self.half)
        core, order = self.core, self.order
        if rows % 16 == 0 and self.half % 128 == 0:
            return Gathered((self.block, self.came, self.low, self.high), shape, order)
        place = owner_slot(core), owner_slot(1 - core)
        own = jnp.take(jnp.concatenate([self.block, self.came]), place[0], axis=0)
        other = jnp.take(jnp.concatenate([self.low, self.high]), place[1], axis=0)
        own = own.reshape(chips * rows, self.half)
        other = other.reshape(chips * rows, self.half)
        full = jnp.where(
            core == 0, jnp.concatenate([own, other], 1), jnp.concatenate([other, own], 1)
        )
        return Gathered((full,), shape)


def add_kernel(count, parts, *refs):
    outs = refs[-parts:]
    at = 0
    for i in range(count):
        keep, came = refs[2 * i : 2 * i + 2]
        spot = slice(at, at + keep.shape[3])
        for j, out in enumerate(outs):
            out[:, :, spot] = (keep[j].astype(F32) + came[j].astype(F32)).astype(BF16)
        at += keep.shape[3]


def add_parts(keeps, cames, parts):
    slots, rows, _ = keeps[0].shape
    size = slots // parts
    steps = 2 if size > 1 else 1
    operands, specs = [], []
    for keep, came in zip(keeps, cames):
        width = keep.shape[2]
        operands += [a.reshape(parts, size, rows, width) for a in (keep, came)]
        specs += [pl.BlockSpec((parts, size // steps, rows, width), lambda i: (0, i, 0, 0))] * 2
    total = sum(k.shape[2] for k in keeps)
    out_spec = pl.BlockSpec((size // steps, rows, total), lambda i: (i, 0, 0))
    return pl.pallas_call(
        functools.partial(add_kernel, len(keeps), parts),
        grid=(steps,),
        in_specs=specs,
        out_specs=[out_spec] * parts,
        out_shape=[jax.ShapeDtypeStruct((size, rows, total), BF16)] * parts,
        compiler_params=params(),
        name="add_parts",
        cost_estimate=cost(1 + total * slots * rows * 1.3e-6),
    )(*operands)


class Scatter:
    def __init__(self, *pairs):
        self.keeps = [keep for _, keep in pairs]
        self.cames = [swap_cores(send) for send, _ in pairs]
        self.stage = stage_count()

    def advance(self, *done):
        kept = self.add(*done)
        return kept if hasattr(self, "total") else self.launch() or kept

    def launch(self, *done):
        partners = stage_partners(self.stage)
        self.cames = [
            swap_chips(after(send, *done) if done else send, masks)
            for send, masks in zip(self.sends, partners)
        ]

    def add(self, *done):
        cames = [after(came, *done) for came in self.cames]
        if self.stage == stage_count() or len(cames) == 1:
            self.stage -= 1
            if self.stage >= 0:
                partners = stage_partners(self.stage)
                keep, *self.sends = add_parts(self.keeps, cames, 1 + len(partners))
                self.keeps = [keep]
                return keep
        total = self.keeps[0].astype(F32)
        for came in cames:
            total = total + came.astype(F32)
        if self.stage > 0:
            self.keeps, self.cames = [total.astype(BF16)], [jnp.zeros_like(total)]
            return self.add()
        self.total = total[0]
        return self.total


def own_rows(part):
    core = lax.axis_index("seq")
    rows = part.shape[0] // 2
    mine = lax.dynamic_slice_in_dim(part, core * rows, rows, axis=0)
    theirs = lax.dynamic_slice_in_dim(part, (1 - core) * rows, rows, axis=0)
    return mine, swap_cores(theirs)


def by_half(mine, came):
    first = lax.axis_index("seq") == 0
    return jnp.concatenate([jnp.where(first, mine, came), jnp.where(first, came, mine)], axis=1)


def look_kernel(codes_ref, table_ref, *refs):
    out_ref, buf, sems = refs[-3:]
    depth = buf.shape[0]
    table_rows = table_ref.shape[0]
    groups = out_ref.shape[0] // 16

    def start(g):
        slot = lax.rem(g, depth)
        for r in range(16):
            code = codes_ref[g * 16 + r]
            code = jnp.where(code < 0, code + table_rows, code)
            code = jnp.where(code >= table_rows, code - table_rows, code)
            first = lax.shift_left(lax.shift_right_logical(code, 4), 4)
            pltpu.make_async_copy(
                table_ref.at[pl.ds(pl.multiple_of(first, 16), 16), :],
                buf.at[slot, pl.ds(16 * r, 16), :],
                sems.at[slot],
            ).start()

    linear = lax.broadcasted_iota(jnp.int32, (16, 256), 0) * 256 + lax.broadcasted_iota(
        jnp.int32, (16, 256), 1
    )

    def finish(g):
        slot = lax.rem(g, depth)
        pick = jnp.zeros((16, 256), jnp.bool_)
        for r in range(16):
            code = codes_ref[g * 16 + r]
            held = (code >= 0) & (code < table_rows)
            pick = pick | (linear == jnp.where(held, r * 256 + r * 16 + (code & 15), -1))
        pltpu.make_async_copy(buf.at[slot], buf.at[slot], sems.at[slot]).wait()
        rows = nn(pick.astype(F32).astype(BF16), buf[slot])
        out_ref[pl.ds(pl.multiple_of(g * 16, 16), 16), :] = rows.astype(BF16)

    for g in range(depth - 1):
        start(jnp.int32(g))

    def step(g, carry):
        @pl.when(g + depth - 1 < groups)
        def _():
            start(g + depth - 1)

        finish(g)
        return carry

    lax.fori_loop(0, groups, step, 0)


def look_up(codes, table, part, parts, into=()):
    count, width = codes.shape[0], table.shape[1]
    depth = 8
    return pl.pallas_call(
        look_kernel,
        grid_spec=pltpu.PrefetchScalarGridSpec(
            num_scalar_prefetch=1,
            grid=(1,),
            in_specs=[ANY] * (1 + len(into)),
            out_specs=pl.BlockSpec((count, width), lambda i, *_: (part, 0)),
            scratch_shapes=[
                pltpu.VMEM((depth, 256, width), BF16),
                pltpu.SemaphoreType.DMA((depth,)),
            ],
        ),
        out_shape=jax.ShapeDtypeStruct((count * parts, width), BF16),
        input_output_aliases={2 + i: i for i in range(len(into))},
        compiler_params=params(),
        name="look_up",
        cost_estimate=cost(count * 0.0187),
    )(codes, table, *into)


def norm_parts(values):
    mean = jnp.mean(values, axis=-1, keepdims=True)
    centred = values - mean
    spread = jnp.mean(centred * centred, axis=-1, keepdims=True)
    inverse = lax.rsqrt(spread + EPS)
    return centred * inverse, inverse


def norm_back(grad, normed, inverse, gain):
    c = grad * gain
    mean = jnp.mean(c, axis=-1, keepdims=True)
    along = jnp.mean(c * normed, axis=-1, keepdims=True)
    return inverse * (c - mean - normed * along)


def gelu_both(u):
    square = u * u
    t = jnp.tanh(u * (GELU_A + (GELU_A * GELU_B) * square))
    half = 0.5 + 0.5 * t
    slope = half + (0.5 * u) * (1.0 - t * t) * (GELU_A + (3 * GELU_A * GELU_B) * square)
    return u * half, slope


def column_sums(values):
    return jnp.sum(values.astype(F32), axis=0, keepdims=True)


def row_block(tile, columns):
    return pl.BlockSpec((tile, columns), lambda i, *_: (i, 0))


def whole(shape):
    return pl.BlockSpec(shape, lambda i, *_: (0,) * len(shape))


def shaped(dtype, *shape):
    return jax.ShapeDtypeStruct(shape, dtype)


def segment_of(position, lengths_ref, batch):
    end = jnp.int32(0)
    segment = jnp.zeros(position.shape, jnp.int32)
    for s in range(lengths_ref.shape[1]):
        end = end + lengths_ref[batch, s]
        segment = segment + (position >= end).astype(jnp.int32)
    return segment


def fill_mask(mask_ref, lengths_ref, core, batch):
    rows = mask_ref.shape[1]
    query = lax.broadcasted_iota(jnp.int32, (1, rows), 1) + core * rows
    query = segment_of(query, lengths_ref, batch)
    for part, owner in enumerate((core, 1 - core)):
        key = lax.broadcasted_iota(jnp.int32, (rows, 128), 0) + owner * rows
        key = segment_of(key, lengths_ref, batch)
        key = jnp.concatenate([key] * (rows // 128), axis=1)
        mask_ref[part * rows : (part + 1) * rows, :] = jnp.where(key == query, 0.0, NEGATIVE)


def head_lanes(block, head):
    lane = lax.broadcasted_iota(jnp.int32, block.shape, 1)
    return jnp.where((lane < HEAD_DIM) == (head == 0), block, jnp.zeros_like(block))


def attend_kernel(
    lengths_ref, core_ref, q_ref, k_ref, v_ref, k2_ref, v2_ref, o_ref, ot_ref, log_ref, mask_ref
):
    k_ref, v_ref, k2_ref, v2_ref = (ref.at[0] for ref in (k_ref, v_ref, k2_ref, v2_ref))
    fill_mask(mask_ref, lengths_ref, core_ref[0], pl.program_id(0))
    pairs = q_ref.shape[1] // 128

    def scores_of(pair):
        at = slice(pair * 128, pair * 128 + 128)
        k = jnp.concatenate([k_ref[:, at], k2_ref[:, at]], axis=0)
        return [nt(k, head_lanes(q_ref[:, at], head)) + mask_ref[...] for head in range(2)]

    ahead = scores_of(0)
    for pair in range(pairs):
        at = slice(pair * 128, pair * 128 + 128)
        values = jnp.concatenate([v_ref[:, at], v2_ref[:, at]], axis=0).T
        outs, scores = [], ahead
        if pair + 1 < pairs:
            ahead = scores_of(pair + 1)
        for head, score in enumerate(scores):
            peak = jnp.max(score, axis=0, keepdims=True)
            expo = jnp.exp(score - peak)
            total = jnp.sum(expo, axis=0, keepdims=True)
            log_ref[0, pair, head : head + 1, :] = peak + jnp.log(total)
            here = slice(head * HEAD_DIM, head * HEAD_DIM + HEAD_DIM)
            outs.append(nn(values[here], expo.astype(BF16)) * (1.0 / total))
        out = jnp.concatenate(outs, axis=0)
        ot_ref[0, at, :] = out
        o_ref[:, at] = out.T.astype(BF16)


def attend(lengths, core, q, kv, kv2):
    micro = lengths.shape[0]
    rows, width = q.shape[0] // micro, q.shape[1]
    pairs = width // 128
    block = row_block(rows, width)
    keys = pl.BlockSpec((1, rows, width), lambda b, *_: (0, b, 0))
    values = pl.BlockSpec((1, rows, width), lambda b, *_: (1, b, 0))
    area = micro * HEADS * rows * 2 * rows
    return pl.pallas_call(
        attend_kernel,
        grid_spec=pltpu.PrefetchScalarGridSpec(
            num_scalar_prefetch=2,
            grid=(micro,),
            in_specs=[block, keys, values, keys, values],
            out_specs=[
                block,
                pl.BlockSpec((1, width, rows), lambda b, *_: (b, 0, 0)),
                pl.BlockSpec((1, pairs, 2, rows), lambda b, *_: (b, 0, 0, 0)),
            ],
            scratch_shapes=[pltpu.VMEM((2 * rows, rows), F32)],
        ),
        out_shape=[
            shaped(BF16, *q.shape),
            shaped(F32, micro, width, rows),
            shaped(F32, micro, pairs, 2, rows),
        ],
        compiler_params=params(),
        name="attend",
        cost_estimate=cost(17),
    )(lengths, core, q, kv, kv, kv2, kv2)


def attend_back_kernel(
    first_batch,
    lengths_ref,
    core_ref,
    q_ref,
    k_ref,
    v_ref,
    k2_ref,
    v2_ref,
    g_ref,
    ot_ref,
    log_ref,
    *refs,
):
    dq_ref, mine_ref, other_ref, mask_ref = refs[-4:]
    rows = q_ref.shape[0]
    k_ref, v_ref, k2_ref, v2_ref = (ref.at[0] for ref in (k_ref, v_ref, k2_ref, v2_ref))
    fill_mask(mask_ref, lengths_ref, core_ref[0], pl.program_id(0) + first_batch)
    for pair in range(q_ref.shape[1] // 128):
        at = slice(pair * 128, pair * 128 + 128)
        q = q_ref[:, at]
        g = g_ref[:, at]
        k = jnp.concatenate([k_ref[:, at], k2_ref[:, at]], axis=0)
        v = jnp.concatenate([v_ref[:, at], v2_ref[:, at]], axis=0)
        keys = k.T
        products = g.astype(F32).T * ot_ref[0, at, :]
        dq, dk, dv = [], 0.0, 0.0
        for head in range(2):
            here = slice(head * HEAD_DIM, head * HEAD_DIM + HEAD_DIM)
            q_head, g_head = head_lanes(q, head), head_lanes(g, head)
            p = jnp.exp(nt(k, q_head) + (mask_ref[...] - log_ref[0, pair, head : head + 1, :]))
            inner = jnp.sum(products[here], axis=0, keepdims=True)
            ds = (p * (nt(v, g_head) - inner)).astype(BF16)
            dq.append(nn(keys[here], ds))
            dk = dk + nn(ds, q_head)
            dv = dv + nn(p.astype(BF16), g_head)
        dq_ref[:, at] = (jnp.concatenate(dq, axis=0).T * SCALE).astype(BF16)
        for i, grad in enumerate((dk, dv)):
            mine_ref[i, :, at] = grad[:rows].astype(BF16)
            other_ref[i, :, at] = grad[rows:].astype(BF16)


def attend_back(lengths, core, q, kv, kv2, g, ot, logs, group, batches, into=()):
    micro = lengths.shape[0]
    rows = q.shape[0] // micro
    first, pairs = group
    width = pairs * 128
    at = first // pairs
    start, stop = batches
    block = pl.BlockSpec((rows, width), lambda b, *_: (b + start, at))
    keys = pl.BlockSpec((1, rows, width), lambda b, *_: (0, b + start, at))
    values = pl.BlockSpec((1, rows, width), lambda b, *_: (1, b + start, at))
    both = pl.BlockSpec((2, rows, width), lambda b, *_: (0, b + start, 0))
    other = pl.BlockSpec((2, rows, width), lambda b, *_: (0, b, 0))
    count = micro * rows
    operands = (lengths, core, q, kv, kv, kv2, kv2, g, ot, logs)
    return pl.pallas_call(
        functools.partial(attend_back_kernel, start),
        grid_spec=pltpu.PrefetchScalarGridSpec(
            num_scalar_prefetch=2,
            grid=(stop - start,),
            in_specs=[
                block,
                keys,
                values,
                keys,
                values,
                block,
                pl.BlockSpec((1, width, rows), lambda b, *_: (b + start, at, 0)),
                pl.BlockSpec((1, pairs, 2, rows), lambda b, *_: (b + start, at, 0, 0)),
            ]
            + [ANY] * len(into),
            out_specs=[pl.BlockSpec((rows, width), lambda b, *_: (b + start, 0)), both, other],
            scratch_shapes=[pltpu.VMEM((2 * rows, rows), F32)],
        ),
        out_shape=[
            shaped(BF16, count, width),
            shaped(BF16, 2, count, width),
            shaped(BF16, 2, (stop - start) * rows, width),
        ],
        input_output_aliases={len(operands) + i: i for i in range(len(into))},
        compiler_params=params(),
        name="attend_back",
        cost_estimate=cost(1.2 * pairs * (stop - start)),
    )(*operands, *into)


def project_kernel(weight_in, order_ref, x_ref, *refs):
    *sources, h_ref, q_ref, kv_ref, vec_ref, full_ref, weight, sems, full_sem = refs
    width = x_ref.shape[1]
    i = pl.program_id(0)
    full_copy = pltpu.make_async_copy(weight, full_ref, full_sem)

    @pl.when(i == 0)
    def _():
        copies = weight_in.copies(order_ref, sources, weight, sems)
        for copy in copies:
            copy.start()
        for copy in copies:
            copy.wait()
        full_copy.start()
        small = weight[:, 3 * width : 3 * width + 128].astype(F32).T
        vec_ref[...] = small[: vec_ref.shape[0]]

    vec = lambda i: vec_ref[i : i + 1, :]
    normed, _ = norm_parts(x_ref[...].astype(F32))
    h = (normed * vec(FIRST_GAIN) + vec(FIRST_BIAS)).astype(BF16)
    h_ref[...] = h
    q = (nn(h, weight[:, :width]) + vec(QUERY_BIAS)).astype(BF16)
    q_ref[...] = (q.astype(F32) * SCALE).astype(BF16)
    kv_ref[0] = nn(h, weight[:, width : 2 * width]).astype(BF16)
    values = nn(h, weight[:, 2 * width : 3 * width]) + vec(VALUE_BIAS)
    kv_ref[1] = values.astype(BF16)

    @pl.when(i == pl.num_programs(0) - 1)
    def _():
        full_copy.wait()


def project(x, weight):
    rows, width = x.shape
    tile = 256
    block = row_block(tile, width)
    return pl.pallas_call(
        functools.partial(project_kernel, weight),
        grid_spec=pltpu.PrefetchScalarGridSpec(
            num_scalar_prefetch=1,
            grid=(rows // tile,),
            in_specs=[block] + weight.specs(),
            out_specs=[
                block,
                block,
                pl.BlockSpec((2, tile, width), lambda i, *_: (0, i, 0)),
                whole((16, width)),
                ANY,
            ],
            scratch_shapes=weight.scratch() + [pltpu.SemaphoreType.DMA],
        ),
        out_shape=[
            shaped(BF16, rows, width),
            shaped(BF16, rows, width),
            shaped(BF16, 2, rows, width),
            shaped(F32, 16, width),
            shaped(BF16, *weight.shape),
        ],
        compiler_params=params(),
        name="project",
        cost_estimate=cost(10),
    )(weight.order, x, *weight.arrays)


def store_rows(ref, slot_ref, first, value, at=0):
    value = value.astype(BF16)
    columns = slice(at, at + value.shape[1])
    if len(ref.shape) == 2:
        ref[:, columns] = value
        return
    chips, rows, _ = ref.shape
    for chip in range(chips):
        ref[slot_ref[first + chip], :, columns] = value[chip * rows : chip * rows + rows]


def by_slots(chips, rows):
    return rows // chips % 16 == 0


def in_slots(product, slots):
    chips = slots.shape[0]
    if product.ndim == 3:
        return product
    product = product.reshape(chips, -1, product.shape[1])
    return jnp.zeros_like(product).at[slots].set(product)


def pair_in_slots(slots, send, keep):
    chips = slots.shape[0] // 2
    return in_slots(send, slots[chips:]), in_slots(keep, slots[:chips])


def product_shape(chips, rows, columns):
    if by_slots(chips, rows):
        return (chips, rows // chips, columns)
    return (rows, columns)


def product_spec(chips, rows, columns, index):
    lead = (0, 0) if by_slots(chips, rows) else (0,)
    return pl.BlockSpec(
        product_shape(chips, rows, columns), lambda i, *_: lead + (index(i),)
    )


def mlp_kernel(
    streams,
    wide_in,
    down_in,
    lengths_ref,
    core_ref,
    slot_ref,
    x_ref,
    o_ref,
    cot_ref,
    near_ref,
    far_ref,
    vec_ref,
    source_ref,
    enc_ref,
    d_ref,
    go_ref,
    down_send_ref,
    down_keep_ref,
    up_send_ref,
    up_keep_ref,
    out_send_ref,
    out_keep_ref,
    db_ref,
    ub_ref,
    gain_ref,
    bias_ref,
    ob_ref,
    wide,
    down,
    active_all,
    upper_all,
    normed_all,
    z_all,
    low_all,
    slope_tile,
    wide_sems,
    down_sems,
):
    i = pl.program_id(0)
    steps = pl.num_programs(0) - active_all.shape[0]
    tiles = lengths_ref.shape[0]
    width = x_ref.shape[1]
    rows = o_ref.shape[0] // tiles
    blocks = active_all.shape[0]
    core = core_ref[0]
    chips = slot_ref.shape[0] // 2
    copies = wide_in.copies(None, [source_ref], wide, wide_sems)
    copies += down_in.copies(None, [source_ref], down, down_sems)

    @pl.when(i == 0)
    def _():
        for copy in copies:
            copy.start()
        for ref in (db_ref, ub_ref, gain_ref, bias_ref, ob_ref):
            ref[...] = jnp.zeros(ref.shape, F32)
        for copy in copies:
            copy.wait()

    def up_columns(b):
        return wide[:, width * (b + 1) : width * (b + 2)]

    def down_rows(b):
        return down[width * b : width * (b + 1), :]

    def stream(k):
        tile = i * streams + k
        here = slice(k * rows, k * rows + rows)
        at = pl.ds(pl.multiple_of(tile * rows, rows), rows)
        vec = lambda k: vec_ref[k : k + 1, :]
        r = x_ref[here, :].astype(F32) + nn(o_ref[at, :], wide[:, :width]) + vec(OUTPUT_BIAS)
        yield
        normed, inverse = norm_parts(r)
        h = (normed * vec(SECOND_GAIN) + vec(SECOND_BIAS)).astype(BF16)
        normed_all[at, :] = h
        yield

        def rise(b):
            return nn(h, up_columns(b)) + vec(UP_BIAS + b)

        upper = rise(0)
        for b in range(blocks):
            now = upper
            if b + 1 < blocks:
                upper = rise(b + 1)
            active, slope = gelu_both(now)
            active_all[b, at, :] = active.astype(BF16)
            slope_tile[k * blocks + b] = slope.astype(BF16)
            yield
        filled = lengths_ref[tile, 0]
        for j in range(1, lengths_ref.shape[1]):
            filled = filled + lengths_ref[tile, j]
        position = lax.broadcasted_iota(jnp.int32, (rows, 1), 0) + core * rows
        live = (position < filled).astype(F32)
        z = r + vec(DOWN_BIAS)
        for b in range(blocks):
            z = z + nn(active_all[b, at, :], down_rows(b))
        yield
        enc_ref[here, :] = (live * z).astype(BF16)
        near, far = near_ref[here, :].astype(F32), far_ref[here, :].astype(F32)
        gz = live * (cot_ref[here, :].astype(F32) + COMMIT * (z - (near + far)))
        low = gz.astype(BF16)
        z_all[at, :] = low
        db_ref[...] += column_sums(low)
        yield
        e = 0.0
        fall = nt(low, down_rows(0))
        for b in range(blocks):
            now = fall
            if b + 1 < blocks:
                fall = nt(low, down_rows(b + 1))
            gu = (now * slope_tile[k * blocks + b].astype(F32)).astype(BF16)
            upper_all[b, at, :] = gu
            ub_ref[:, width * b : width * (b + 1)] += column_sums(gu)
            e = e + nt(gu, up_columns(b))
            yield
        gain_ref[...] += column_sums(e * normed)
        bias_ref[...] += column_sums(e)
        d = gz + norm_back(e, normed, inverse, vec(SECOND_GAIN))
        d_ref[here, :] = d
        low = d.astype(BF16)
        low_all[at, :] = low
        ob_ref[...] += column_sums(low)
        yield
        go_ref[here, :] = nt(low, wide[:, :width]).astype(BF16)

    @pl.when(i < steps)
    def _():
        running = [stream(k) for k in range(streams)]
        while running:
            running = [each for each in running if next(each, "end") != "end"]

    def split(out, send_ref, keep_ref):
        half = out.shape[1] // 2
        first = core == 0
        store_rows(keep_ref, slot_ref, 0, jnp.where(first, out[:, :half], out[:, half:]))
        store_rows(send_ref, slot_ref, chips, jnp.where(first, out[:, half:], out[:, :half]))

    @pl.when(i >= steps)
    def _():
        j = i - steps
        split(tn(active_all[j], z_all[...]), down_send_ref, down_keep_ref)
        column = lax.rem(j + blocks // 2 * (1 - core), blocks)
        product = tn(normed_all[...], upper_all[column])

        @pl.when(j < blocks // 2)
        def _():
            store_rows(up_send_ref, slot_ref, chips, product)

        @pl.when(j >= blocks // 2)
        def _():
            store_rows(up_keep_ref, slot_ref, 0, product)

    @pl.when(i == steps + blocks - 1)
    def _():
        split(tn(o_ref[...], low_all[...]), out_send_ref, out_keep_ref)


def mlp(lengths, core, slots, x, o, cot, near, far, vec, wide, down):
    rows, width = x.shape
    hidden = down.shape[0]
    tiles, blocks = lengths.shape[0], hidden // width
    tile = rows // tiles
    streams = 1
    steps = tiles // streams
    chips = slots.shape[0] // 2
    block = pl.BlockSpec(
        (streams * tile, width), lambda i, *_: (jnp.minimum(i, steps - 1), 0)
    )
    row, long_row = whole((1, width)), whole((1, hidden))
    down_spec = product_spec(chips, width, width // 2, lambda i: jnp.maximum(i - steps, 0))
    send_spec = product_spec(chips, width, width, lambda i: jnp.clip(i - steps, 0, blocks // 2 - 1))
    keep_spec = product_spec(chips, width, width, lambda i: jnp.maximum(i - steps - blocks // 2, 0))
    out_spec = product_spec(chips, width, width // 2, lambda i: 0)
    half_hidden = shaped(BF16, *product_shape(chips, width, hidden // 2))
    half_width = shaped(BF16, *product_shape(chips, width, width // 2))
    results = pl.pallas_call(
        functools.partial(mlp_kernel, streams, wide, down),
        grid_spec=pltpu.PrefetchScalarGridSpec(
            num_scalar_prefetch=3,
            grid=(steps + blocks,),
            in_specs=[block, whole(o.shape), block, block, block]
            + [whole(vec.shape), ANY],
            out_specs=[block, block, block]
            + [down_spec, down_spec, send_spec, keep_spec, out_spec, out_spec]
            + [row, long_row, row, row, row],
            scratch_shapes=[
                pltpu.VMEM(wide.shape, BF16),
                pltpu.VMEM(down.shape, BF16),
                pltpu.VMEM((blocks, rows, width), BF16),
                pltpu.VMEM((blocks, rows, width), BF16),
                pltpu.VMEM((rows, width), BF16),
                pltpu.VMEM((rows, width), BF16),
                pltpu.VMEM((rows, width), BF16),
                pltpu.VMEM((streams * blocks, tile, width), BF16),
                pltpu.SemaphoreType.DMA((blocks,)),
                pltpu.SemaphoreType.DMA((blocks,)),
            ],
        ),
        out_shape=[
            shaped(BF16, rows, width),
            shaped(F32, rows, width),
            shaped(BF16, rows, width),
            half_hidden,
            half_hidden,
            half_hidden,
            half_hidden,
            half_width,
            half_width,
            shaped(F32, 1, width),
            shaped(F32, 1, hidden),
            shaped(F32, 1, width),
            shaped(F32, 1, width),
            shaped(F32, 1, width),
        ],
        compiler_params=params(),
        name="mlp",
        cost_estimate=cost(55),
    )(lengths, core, slots, x, o, cot, near, far, vec, *wide.arrays)
    down_pair, up_pair, out_pair = (pair_in_slots(slots, *results[k : k + 2]) for k in (3, 5, 7))
    return results[:3], down_pair, up_pair, out_pair, results[9:]


def leave_kernel(group, last, core_ref, slot_ref, *refs):
    refs = list(refs)
    take = lambda count: [refs.pop(0) for _ in range(count)]
    dq_ref, mine_ref, came_ref, late_ref, h_ref, full_ref = take(6)
    if last:
        e_in_ref, d_ref, x_ref, vec_ref, small_ref = take(5)
        send_ref, keep_ref, dx_ref = take(3)
        sums = take(1)[0]
    else:
        send_ref, keep_ref, e_ref, sums = take(4)
    weight, grads, sems = refs
    first, pairs = group
    size = pairs * 128
    i = pl.program_id(0)
    rows = dq_ref.shape[0]
    width = h_ref.shape[1]
    core = core_ref[0]
    chips = slot_ref.shape[0] // 2
    copies = []
    for part in range(3):
        source = full_ref.at[:, pl.ds(part * width + first * 128, size)]
        spot = weight.at[:, pl.ds(part * size, size)]
        copies.append(pltpu.make_async_copy(source, spot, sems.at[part]))

    @pl.when(i == 0)
    def _():
        for copy in copies:
            copy.start()
        for copy in copies:
            copy.wait()
        sums[...] = jnp.zeros(sums.shape, F32)

    @pl.when(i < pl.num_programs(0) - 1)
    def _():
        at = pl.ds(pl.multiple_of(i * rows, rows), rows)
        here = slice(first * 128, first * 128 + size)
        dq = dq_ref[...]
        parts = [dq]
        early = i < (pl.num_programs(0) - 1) // 2
        for k in range(2):
            came = jnp.where(early, came_ref[k], late_ref[k])
            total = mine_ref[k].astype(F32) + came.astype(F32)
            parts.append(total.astype(BF16))
        sums[QUERY_BIAS : QUERY_BIAS + 1, here] += column_sums(dq)
        sums[VALUE_BIAS : VALUE_BIAS + 1, here] += column_sums(parts[2])
        grad = jnp.concatenate(parts, axis=1)
        half = grad.shape[1] // 2
        grads[0, at, :] = grad[:, :half]
        grads[1, at, :] = grad[:, half:]
        e = nt(grad, weight[...])
        if last:
            e = e + e_in_ref[...]
            normed, inverse = norm_parts(x_ref[...].astype(F32))
            sums[FIRST_GAIN : FIRST_GAIN + 1, :] += column_sums(e * normed)
            sums[FIRST_BIAS : FIRST_BIAS + 1, :] += column_sums(e)
            back = norm_back(e, normed, inverse, vec_ref[FIRST_GAIN : FIRST_GAIN + 1, :])
            dx_ref[...] = (d_ref[...] + back).astype(BF16)
        else:
            e_ref[...] = e

    @pl.when(i == pl.num_programs(0) - 1)
    def _():
        store_rows(send_ref, slot_ref, chips, tn(h_ref[...], grads[1 - core]))
        store_rows(keep_ref, slot_ref, 0, tn(h_ref[...], grads[core]))
        if last:
            small = sums[...] + small_ref[...]
            small = jnp.concatenate([small, jnp.zeros((SMALL // 2 - 16, width), F32)]).T
            store_rows(send_ref, slot_ref, chips, small, grads.shape[2])
            store_rows(keep_ref, slot_ref, 0, small, grads.shape[2])


def leave(group, core, slots, dq, mine, came, h, full, *rest):
    rows, width = h.shape
    size = dq.shape[1]
    last = bool(rest)
    tile = 256
    tiles = rows // tile
    chips = slots.shape[0] // 2
    half = 3 * size // 2
    columns = half + (SMALL // 2 if last else 0)

    def part(columns):
        return pl.BlockSpec((tile, columns), lambda i, *_: (jnp.minimum(i, tiles - 1), 0))

    both = pl.BlockSpec((2, tile, size), lambda i, *_: (0, jnp.minimum(i, tiles - 1), 0))
    half_tiles = tiles // 2
    early = pl.BlockSpec(
        (2, tile, size), lambda i, *_: (0, jnp.minimum(i, half_tiles - 1), 0)
    )
    late = pl.BlockSpec(
        (2, tile, size),
        lambda i, *_: (0, jnp.clip(i - half_tiles, 0, half_tiles - 1), 0),
    )
    block = part(width)
    in_specs = [part(size), both, early, late, whole(h.shape), ANY]
    if last:
        in_specs += [block, block, block, whole(rest[3].shape), whole(rest[4].shape)]
    product = product_spec(chips, width, columns, lambda i: 0)
    product_out = shaped(BF16, *product_shape(chips, width, columns))
    send, keep, out, sums = pl.pallas_call(
        functools.partial(leave_kernel, group, last),
        grid_spec=pltpu.PrefetchScalarGridSpec(
            num_scalar_prefetch=2,
            grid=(tiles + 1,),
            in_specs=in_specs,
            out_specs=[product, product, block, whole((16, width))],
            scratch_shapes=[
                pltpu.VMEM((width, 3 * size), BF16),
                pltpu.VMEM((2, rows, half), BF16),
                pltpu.SemaphoreType.DMA((3,)),
            ],
        ),
        out_shape=[
            product_out,
            product_out,
            shaped(BF16 if last else F32, rows, width),
            shaped(F32, 16, width),
        ],
        compiler_params=params(),
        name="leave",
        cost_estimate=cost(13),
    )(core, slots, dq, mine, *came, h, full, *rest)
    return pair_in_slots(slots, send, keep), out, sums


def body(
    patches,
    code_index,
    lengths,
    cotangent,
    codebook,
    first_gain,
    first_bias,
    project_weight,
    query_bias,
    value_bias,
    output_weight,
    output_bias,
    second_gain,
    second_bias,
    up_weight,
    up_bias,
    down_weight,
    down_bias,
):
    micro, _, local_rows, width = patches.shape
    rows = micro * local_rows
    hidden = up_weight.shape[1]
    place = lax.axis_index("seq")
    core = place.reshape(1).astype(jnp.int32)
    lengths = lengths[:, 0]
    shard_rows = project_weight.shape[0]
    spread = hidden // width

    small = [
        first_gain,
        first_bias,
        query_bias,
        value_bias,
        output_bias,
        second_gain,
        second_bias,
        down_bias,
    ]
    small += [up_bias[j * shard_rows : (j + 1) * shard_rows] for j in range(spread)]
    line = lax.broadcasted_iota(jnp.int32, (16, shard_rows), 0)
    table = jnp.zeros((16, shard_rows), BF16)
    for j, vector in enumerate(small):
        table = jnp.where(line == j, vector[None, :], table)
    small = jnp.pad(table.T, ((0, 0), (0, SMALL - 16)))
    g1 = Gather(jnp.concatenate([project_weight, small], axis=1))
    inputs = patches.reshape(rows, width)
    cotan = cotangent.reshape(rows, width)
    codes = code_index.reshape(-1)
    local = codes - place * codebook.shape[0]
    asked = swap_cores(codes) - place * codebook.shape[0]
    piece = rows // 2
    asked = [asked[i : i + piece] for i in range(0, rows, piece)]
    local = [local[i : i + piece] for i in range(0, rows, piece)]

    looked = []

    def look(*done):
        at = len(looked)
        codes = after((asked + local)[at], *looked[-1:], *done)
        into = looked[-1:] if at % 2 else ()
        looked.append(look_up(codes, codebook, at % 2, 2, into))
        return looked[-1]

    block1 = g1.advance()
    up_shard = after(up_weight, block1).reshape(shard_rows, -1, spread, shard_rows)
    up_shard = up_shard.transpose(0, 2, 1, 3).reshape(shard_rows, hidden)
    down_shard = [down_weight[j * shard_rows : (j + 1) * shard_rows] for j in range(spread)]
    beside = jnp.concatenate([output_weight, up_shard, *down_shard], axis=1)
    gathered = lax.all_gather(beside, BOTH, axis=0, tiled=True)
    wide_all = Gathered((gathered,), (width, width + hidden))
    down_all = Gathered((gathered,), (hidden, width), first=width + hidden)
    slots = jnp.concatenate([owner_slot(place), owner_slot(1 - place)])
    block1 = g1.advance(look(beside, slots, g1.order))
    block1 = g1.advance(look(block1))
    g1.advance(look(block1))
    project_all = g1.result()

    normed, q, kv, vec, project_full = project(inputs, project_all)
    kv2 = swap_cores(kv)
    look(q)
    far, near = swap_cores(looked[1]), looked[3]
    mixed, mixed_t, logs = attend(lengths, core, after(q, near), kv, kv2)
    (encoded, grad_resid, mixed_grad), down_pair, up_pair, out_pair, sums = mlp(
        lengths, core, slots, inputs, mixed, cotan, near, far, vec, wide_all, down_all
    )
    grad_down_bias, grad_up_bias, grad_second_gain, grad_second_bias, grad_output_bias = sums
    mlp_sums = Scatter(down_pair, up_pair)

    def back(group, batches, *done, into=()):
        return attend_back(
            lengths,
            core,
            after(q, *done),
            kv,
            kv2,
            mixed_grad,
            mixed_t,
            logs,
            group,
            batches,
            into,
        )

    early = back(GROUPS[0], (0, micro // 2))
    kept = mlp_sums.advance(early[0])
    came = [swap_cores(early[2])]
    dq, mine, other = back(GROUPS[0], (micro // 2, micro), kept, into=early[:2])
    came.append(swap_cores(other))
    pair, partial, small = leave(
        GROUPS[0], core, slots, dq, mine, came, normed, project_full
    )
    kept = mlp_sums.advance(*pair)
    first_sums = Scatter(*[(after(send, kept), keep) for send, keep in (out_pair, pair)])
    early = back(GROUPS[1], (0, micro // 2), kept)
    kept = first_sums.advance(early[0])
    came2 = [swap_cores(early[2])]
    dq2, mine2, other2 = back(GROUPS[1], (micro // 2, micro), kept, into=early[:2])
    came2.append(swap_cores(other2))
    rest = [
        jnp.zeros((OUTPUT_BIAS, width), F32),
        grad_output_bias,
        grad_second_gain,
        grad_second_bias,
        grad_down_bias,
        grad_up_bias.reshape(spread, width),
        jnp.zeros((16 - UP_BIAS - spread, width), F32),
    ]
    small = small + jnp.concatenate(rest)
    kept = mlp_sums.advance(dq2)
    kept = first_sums.advance(kept, small)
    second_pair, grad_inputs, _ = leave(
        GROUPS[1],
        core,
        slots,
        after(dq2, kept),
        mine2,
        came2,
        normed,
        project_full,
        partial,
        grad_resid,
        inputs,
        vec,
        small,
    )
    second_sums = Scatter(second_pair)

    def finish(sums, kept):
        while not hasattr(sums, "total"):
            kept = sums.advance(kept)
        return kept

    half = width // 2

    def columns(pair, first, count):
        return by_half(*[part[:, first : first + count] for part in pair])

    kept = finish(mlp_sums, grad_inputs)
    kept = second_sums.advance(kept)
    kept = first_sums.advance(kept)
    kept = second_sums.advance(kept)
    pair = own_rows(after(mlp_sums.total, kept))
    grad_down = jnp.concatenate([columns(pair, j * half, half) for j in range(spread)])
    grad_up = columns(pair, spread * half, hidden // 2)
    grad_up = grad_up.reshape(shard_rows, spread, -1, shard_rows).transpose(0, 2, 1, 3)
    grad_up = grad_up.reshape(shard_rows, hidden)
    kept = second_sums.advance(kept, grad_up, grad_down)
    kept = finish(first_sums, kept)
    finish(second_sums, kept)
    pair = own_rows(first_sums.total)
    grad_output = columns(pair, 0, half)
    parts = [columns(pair, half, first_sums.total.shape[1] - half)]
    size = second_sums.total.shape[1] - SMALL // 2
    parts.append(by_half(*own_rows(second_sums.total[:, :size])))
    grad_small = second_sums.total[:, size:]
    grad_small = lax.dynamic_slice_in_dim(grad_small, place * shard_rows, shard_rows, axis=0)
    grad_project_weight = jnp.concatenate(
        [
            part[:, i * pairs * 128 : (i + 1) * pairs * 128]
            for i in range(3)
            for (_, pairs), part in zip(GROUPS, parts)
        ],
        axis=1,
    )
    (
        grad_first_gain,
        grad_first_bias,
        grad_query_bias,
        grad_value_bias,
        grad_output_bias,
        grad_second_gain,
        grad_second_bias,
        grad_down_bias,
    ) = grad_small[:, :UP_BIAS].T
    grad_up_bias = grad_small[:, UP_BIAS : UP_BIAS + spread].T.reshape(-1)

    shape = patches.shape
    return (
        encoded.reshape(shape),
        grad_inputs.reshape(shape),
        grad_first_gain,
        grad_first_bias,
        grad_project_weight,
        grad_query_bias,
        grad_value_bias,
        grad_output,
        grad_output_bias,
        grad_second_gain,
        grad_second_bias,
        grad_up,
        grad_up_bias,
        grad_down,
        grad_down_bias,
    )


def solution(mesh):
    split = P(BOTH)
    split_rows = P(BOTH, None)
    patch = P(None, "dp", "seq", None)
    placed = (
        patch,
        P(None, "dp", "seq"),
        P(None, "dp", None),
        patch,
        P("seq", None),
        split,
        split,
        split_rows,
        split,
        split,
        split_rows,
        split,
        split,
        split,
        split_rows,
        split,
        split_rows,
        split,
    )
    return jax.shard_map(
        body,
        mesh=mesh,
        in_specs=placed,
        out_specs=(
            patch,
            patch,
            split,
            split,
            split_rows,
            split,
            split,
            split_rows,
            split,
            split,
            split,
            split_rows,
            split,
            split_rows,
            split,
        ),
        check_vma=False,
    )
```
